256 devices in a mesh: row: 16 (over y_hi, x, core), rep: 16 (over y_lo, z).
Axes of the slice: x: 4, y: 4 (y_hi: 2, y_lo: 2; y = y_hi * 2 + y_lo), z: 8, core: 2. Of those that a mesh axis runs over, the one named last changes fastest.
Arguments:
- features: bfloat16 [65536, 512], P(('row', 'rep')), may hold values from -6 to 6
- tiles: bfloat16 [512, 8, 128, 128], P(('row', 'rep')), may hold values from -0.1875 to 0.1875
- columns: int32 [512, 8], P(('row', 'rep')), may hold values from 0 to 511, as said below
- w_aggregate: bfloat16 [512, 512], replicated, may hold values from -0.25 to 0.25
- w_self: bfloat16 [512, 512], replicated, may hold values from -0.25 to 0.25
- w_middle: bfloat16 [512, 512], replicated, may hold values from -0.25 to 0.25
- w_output: bfloat16 [512, 512], replicated, may hold values from -0.25 to 0.25
- cotangent: bfloat16 [65536, 512], P(('row', 'rep')), may hold values from -6 to 6
Outputs:
- updated: bfloat16 [65536, 512], P(('row', 'rep'))
- grad_features: bfloat16 [65536, 512], P(('row', 'rep'))
- grad_output: float32 [512, 512], P('rep')
- grad_middle: float32 [512, 512], P('rep')
- grad_aggregate: float32 [512, 512], P('rep')
- grad_self: float32 [512, 512], P('rep')
The draws below stay inside these ranges and needn't reach their ends.
Inputs may be any that keep to these rules, and one draw needn't show every extreme that they name: `columns`: row group g holds row blocks g * 32 to (g + 1) * 32 - 1, for g < 16. Every column block named by a row block of group g lies in group g - 1, g or g + 1, taken modulo 16; every row block names each of these three groups at least once. Column blocks may repeat within a row block.
All inputs are finite; a program needn't handle non-finite values.
Results may differ from the reference program's by a relative error of at most 0.015.
Values may be sent and summed in bfloat16 or wider, within the bound.
A program may use at most 192 MiB of HBM per device.

```python
import jax
import jax.numpy as jnp

F = 512
TILE = 128
K = 8
GROUPS = 16
PANEL_BLOCKS = 32
BLOCKS = 512
NODES = 65536


def draw_columns(key, part):
    key_offset, key_within = jax.random.split(key)
    block_ids = jnp.arange(BLOCKS, dtype=jnp.int32)
    group_ids = block_ids // PANEL_BLOCKS
    random_offset = jax.random.randint(key_offset, (BLOCKS, K), -1, 2, dtype=jnp.int32)
    position = jnp.arange(K, dtype=jnp.int32)[None, :]
    offset = jnp.where(position == 0, -1, jnp.where(position == 1, 1, jnp.where(position == 2, 0, random_offset)))
    within = jax.random.randint(key_within, (BLOCKS, K), 0, PANEL_BLOCKS, dtype=jnp.int32)
    target = (group_ids[:, None] + offset + GROUPS) % GROUPS
    return (target * PANEL_BLOCKS + within).astype(jnp.int32)


def shard_levels(own_key, dims, shards, low, high):
    loudness = 1.0
    for dim, blocks in shards:
        steps = jax.random.uniform(jax.random.fold_in(jax.random.fold_in(own_key, 6), dim), (blocks,), jnp.float32, low / len(shards), high / len(shards))
        loudness = loudness * jnp.repeat(jnp.exp(steps), dims[dim] // blocks).reshape((-1,) + (1,) * (len(dims) - 1 - dim))
    return loudness


def gaussian(key, shape, scale, limit, cuts=(), kind=jnp.bfloat16):
    factor_of = shard_levels(key, shape, cuts, -0.22, 0.18) if cuts else 1.0
    result = jax.random.normal(key, shape, jnp.float32) * scale * factor_of
    return jnp.minimum(jnp.maximum(result, -limit), limit).astype(kind)


def setup_inputs(seed: int = 0) -> dict:
    streams_of = jax.random.split(jax.random.key(seed), 9)
    features = gaussian(streams_of[0], (NODES, F), 1.0, 6.0, ((0, 256),))
    tiles = gaussian(streams_of[1], (BLOCKS, K, TILE, TILE), (K * TILE) ** -0.5, 0.1875, ((0, 256),))
    columns = draw_columns(jax.random.fold_in(streams_of[8], 71), 0)
    w_aggregate = gaussian(streams_of[3], (F, F), F ** -0.5, 0.25)
    w_self = gaussian(streams_of[4], (F, F), F ** -0.5, 0.25)
    w_middle = gaussian(streams_of[5], (F, F), F ** -0.5, 0.25)
    w_output = gaussian(streams_of[6], (F, F), F ** -0.5, 0.25)
    cotangent = gaussian(streams_of[7], (NODES, F), 1.0, 6.0, ((0, 256),))
    return dict(features=features, tiles=tiles, columns=columns, w_aggregate=w_aggregate, w_self=w_self, w_middle=w_middle, w_output=w_output, cotangent=cotangent)


def silu_slope(value):
    sig = jax.nn.sigmoid(value)
    return sig * (1.0 + value * (1.0 - sig))


def reference(features, tiles, columns, w_aggregate, w_self, w_middle, w_output, cotangent):
    node_blocks = features.reshape(BLOCKS, TILE, F)
    summed = jnp.zeros((BLOCKS, TILE, F), jnp.float32)
    for column in range(K):
        picked = node_blocks[columns[:, column]].astype(jnp.float32)
        summed = summed + jnp.einsum("bij,bjf->bif", tiles[:, column].astype(jnp.float32), picked)
    aggregate = summed.reshape(NODES, F).astype(jnp.bfloat16)
    pre_first = jnp.dot(aggregate, w_aggregate, preferred_element_type=jnp.float32) + jnp.dot(features, w_self, preferred_element_type=jnp.float32)
    first = jax.nn.silu(pre_first).astype(jnp.bfloat16)
    pre_second = jnp.dot(first, w_middle, preferred_element_type=jnp.float32)
    second = jax.nn.silu(pre_second).astype(jnp.bfloat16)
    updated = (features.astype(jnp.float32) + jnp.dot(second, w_output, preferred_element_type=jnp.float32)).astype(jnp.bfloat16)
    delta_second = (jnp.dot(cotangent, w_output.T, preferred_element_type=jnp.float32) * silu_slope(pre_second)).astype(jnp.bfloat16)
    delta_first = (jnp.dot(delta_second, w_middle.T, preferred_element_type=jnp.float32) * silu_slope(pre_first)).astype(jnp.bfloat16)
    delta_aggregate = jnp.dot(delta_first, w_aggregate.T, preferred_element_type=jnp.float32).astype(jnp.bfloat16)
    delta_blocks = delta_aggregate.reshape(BLOCKS, TILE, F).astype(jnp.float32)
    returned = jnp.zeros((BLOCKS, TILE, F), jnp.float32)
    for column in range(K):
        message = jnp.einsum("bji,bjf->bif", tiles[:, column].astype(jnp.float32), delta_blocks)
        returned = returned.at[columns[:, column]].add(message)
    grad_features = (cotangent.astype(jnp.float32) + jnp.dot(delta_first, w_self.T, preferred_element_type=jnp.float32) + returned.reshape(NODES, F)).astype(jnp.bfloat16)
    scale = 1.0 / (NODES ** 0.5)
    grad_output = jnp.dot(second.T, cotangent, preferred_element_type=jnp.float32) * scale
    grad_middle = jnp.dot(first.T, delta_second, preferred_element_type=jnp.float32) * scale
    grad_aggregate = jnp.dot(aggregate.T, delta_first, preferred_element_type=jnp.float32) * scale
    grad_self = jnp.dot(features.T, delta_first, preferred_element_type=jnp.float32) * scale
    return (updated, grad_features, grad_output, grad_middle, grad_aggregate, grad_self)
```

```python
import math

import jax
import jax.numpy as jnp
from jax import lax
from jax.experimental import pallas as pl
from jax.experimental.pallas import tpu as pltpu
from jax.sharding import PartitionSpec as P

MESH = pl.DeviceIdType.MESH
BF = jnp.bfloat16
F32 = jnp.float32
VMEM = pltpu.VMEM
DMA = pltpu.SemaphoreType.DMA


def wrap16(value):
    return lax.rem(value + 16, 16)


def quarter(rep):
    return (rep // 8) * 2 + rep % 2


def mate(rep, core, part):
    z = rep % 8
    step = jnp.where((z + core) % 2 == 0, 1, 7)
    other = (z + step) % 8
    return (part // 2) * 8 + jnp.where(z % 2 == part % 2, z, other)


def lanes(part, size=128):
    return pl.ds(pl.multiple_of(part * size, size), size)


def remote(src, dst, send, recv, row, rep):
    return pltpu.make_async_remote_copy(
        src_ref=src, dst_ref=dst, send_sem=send, recv_sem=recv, device_id=(row, rep), device_id_type=MESH
    )


def window_index(column, group):
    panel = jnp.minimum(lax.rem(lax.div(column, 32) - group + 17, 16), 2)
    return panel * 32 + lax.rem(column, 32)


def dot(a, b):
    return jnp.dot(a, b, preferred_element_type=F32)


def dot_bt(a, b):
    return lax.dot_general(a, b, (((1,), (1,)), ((), ())), preferred_element_type=F32)


def dot_at(a, b):
    return lax.dot_general(a, b, (((0,), (0,)), ((), ())), preferred_element_type=F32)


def silu_slope(value):
    sig = jax.nn.sigmoid(value)
    return sig * (1.0 + value * (1.0 - sig))


def greet(peers):
    barrier = pltpu.get_barrier_semaphore()
    for row, rep in peers:
        pl.semaphore_signal(barrier, inc=1, device_id=(row, rep), device_id_type=MESH)
    pl.semaphore_wait(barrier, len(peers))


def forward_kernel(
    feat, tiles, cols, w_agg, w_self, w_mid, w_out, cot,
    upd, base, tiles_t, cols_t, delt, grads,
    win, cols_s, aggq, aggr, dagg, self_part, cot_part,
    loc, s1, r1, sx, rx, st, rt, sc, rc, sa, ra, sd, rd,
):
    g = lax.axis_index("row")
    r = lax.axis_index("rep")
    core = g % 2
    f = quarter(r)
    up, down = wrap16(g + 1), wrap16(g - 1)
    greet([(g, wrap16(r + o)) for o in range(1, 16)] + [(up, r), (down, r)])

    def slot(panel, rep):
        return win.at[pl.ds(panel * 32 + rep * 2, 2)]

    def plane_copy(o):
        peer = wrap16(r + o)
        return remote(
            feat.at[:, :, lanes(quarter(peer))], slot(1, r), s1.at[o], r1.at[o], g, peer
        )

    def plane_arrival(o):
        src = wrap16(r - o)
        return remote(slot(1, src), slot(1, src), s1.at[o], r1.at[o], g, src)

    def ring_copies(o):
        src = wrap16(r - o)
        return (
            remote(slot(1, src), slot(0, src), sx.at[0, o], rx.at[0, o], up, r),
            remote(slot(1, src), slot(2, src), sx.at[1, o], rx.at[1, o], down, r),
        )

    def ring_arrivals(o):
        src = wrap16(r - o)
        return (
            remote(slot(0, src), slot(0, src), sx.at[0, o], rx.at[0, o], down, r),
            remote(slot(2, src), slot(2, src), sx.at[1, o], rx.at[1, o], up, r),
        )

    def team(j):
        part = (f + j) % 4
        return part, mate(r, core, part)

    own = pltpu.make_async_copy(feat.at[:, :, lanes(f)], slot(1, r), loc.at[0])
    own.start()
    own_tiles = pltpu.make_async_copy(tiles, tiles_t.at[pl.ds(f * 16, 16)], loc.at[1])
    own_tiles.start()
    own_cols = pltpu.make_async_copy(cols, cols_t.at[f], loc.at[2])
    own_cols.start()

    @pl.loop(1, 16)
    def _(o):
        plane_copy(o).start()

    def tile_copy(j):
        peer = team(j)[1]
        return (
            remote(cols, cols_t.at[f], sc.at[j], rc.at[j], g, peer),
            remote(tiles, tiles_t.at[pl.ds(f * 16, 16)], st.at[j], rt.at[j], g, peer),
        )

    def tile_arrival(j):
        part, peer = team(4 - j)
        return (
            remote(cols_t.at[part], cols_t.at[part], sc.at[j], rc.at[j], g, peer),
            remote(
                tiles_t.at[pl.ds(part * 16, 16)], tiles_t.at[pl.ds(part * 16, 16)], st.at[j], rt.at[j], g, peer
            ),
        )

    for j in range(1, 4):
        for copy in tile_copy(j):
            copy.start()
    own.wait()
    for copy in ring_copies(0):
        copy.start()

    feat2 = feat[...].reshape(256, 512)
    cot2 = cot[...]
    self_part[...] = dot(feat2, w_self[...])
    cot_part[...] = dot_bt(cot2, w_out[...])

    @pl.loop(1, 16)
    def _(o):
        plane_arrival(o).wait_recv()
        for copy in ring_copies(o):
            copy.start()

    own_cols.wait()
    for j in range(1, 4):
        tile_arrival(j)[0].wait_recv()
    to_smem = pltpu.make_async_copy(cols_t, cols_s, loc.at[3])
    to_smem.start()
    to_smem.wait()
    own_tiles.wait()
    for j in range(1, 4):
        tile_arrival(j)[1].wait_recv()

    @pl.loop(0, 16)
    def _(o):
        for copy in ring_arrivals(o):
            copy.wait_recv()

    def agg_copy(j):
        part, peer = team(j)
        return remote(
            aggq.at[pl.ds(part * 2, 2)], aggr.at[:, :, lanes(f)], sa.at[j], ra.at[j], g, peer
        )

    def agg_arrival(j):
        part, peer = team(4 - j)
        view = aggr.at[:, :, lanes(part)]
        return remote(view, view, sa.at[j], ra.at[j], g, peer)

    def block_sum(part, half):
        picked = []
        for k in range(8):
            c = cols_s[part, half, k]
            index = window_index(c, g)
            picked.append(win[index])
        left = jnp.concatenate([tiles_t[part * 16 + half * 8 + k] for k in range(8)], axis=1)
        return dot(left, jnp.concatenate(picked, axis=0)).astype(BF)

    for j in (1, 2, 3, 0):
        part, peer = team(j)
        for half in range(2):
            total = block_sum(part, half)
            if j:
                aggq[part * 2 + half] = total
            else:
                aggr[half, :, lanes(f)] = total
        if j:
            agg_copy(j).start()
    for j in range(1, 4):
        agg_arrival(j).wait_recv()

    agg = aggr[...].reshape(256, 512)
    pre_first = dot(agg, w_agg[...]) + self_part[...]
    first = (pre_first * jax.nn.sigmoid(pre_first)).astype(BF)
    pre_second = dot(first, w_mid[...])
    second = (pre_second * jax.nn.sigmoid(pre_second)).astype(BF)
    delta_second = (cot_part[...] * silu_slope(pre_second)).astype(BF)
    delta_first = (dot_bt(delta_second, w_mid[...]) * silu_slope(pre_first)).astype(BF)
    dagg[...] = dot_bt(delta_first, w_agg[...]).astype(BF).reshape(2, 128, 512)

    def delta_copy(j):
        part, peer = team(j)
        return remote(
            dagg.at[:, :, lanes(part)], delt.at[pl.ds(f * 2, 2)], sd.at[j], rd.at[j], g, peer
        )

    def delta_arrival(j):
        part, peer = team(4 - j)
        view = delt.at[pl.ds(part * 2, 2)]
        return remote(view, view, sd.at[j], rd.at[j], g, peer)

    for j in range(1, 4):
        delta_copy(j).start()
    delt[pl.ds(f * 2, 2)] = dagg[:, :, lanes(f)]
    upd[...] = (feat2.astype(F32) + dot(second, w_out[...])).astype(BF)
    base[...] = (cot2.astype(F32) + dot_bt(delta_first, w_self[...])).reshape(2, 128, 512)
    grads[0] = dot_at(second, cot2).astype(BF)
    grads[1] = dot_at(first, delta_second).astype(BF)
    grads[2] = dot_at(agg, delta_first).astype(BF)
    grads[3] = dot_at(feat2, delta_first).astype(BF)
    for j in range(1, 4):
        delta_arrival(j).wait_recv()

    @pl.loop(1, 16)
    def _(o):
        plane_copy(o).wait_send()

    @pl.loop(0, 16)
    def _(o):
        for copy in ring_copies(o):
            copy.wait_send()

    for j in range(1, 4):
        for copy in tile_copy(j):
            copy.wait_send()
        agg_copy(j).wait_send()
        delta_copy(j).wait_send()


def spread_kernel(cols_s, group, tiles_t, delt, out, acc):
    g = group[0]

    @pl.loop(0, 96)
    def _(i):
        acc[i] = jnp.zeros((128, 128), F32)

    @pl.loop(0, 8)
    def _(i):
        delta = delt[i]
        for k in range(8):
            c = cols_s[i * 8 + k]
            index = window_index(c, g)
            acc[index] += dot_at(tiles_t[i * 8 + k], delta)

    @pl.loop(0, 96)
    def _(i):
        out[i] = acc[i].astype(BF)


def return_kernel(
    scale,
    msgs, base, grads,
    gf, gout,
    from_prior, from_next, sums, parts, half_in, half, ring_in, ring, pair_in, pair, rep_in, piece,
    sx, rx, sp, rp, s_core, r_core, s_ring, r_ring, s_pair, r_pair, s_rep, r_rep, s_row, r_row,
):
    g = lax.axis_index("row")
    r = lax.axis_index("rep")
    core = g % 2
    x = (g // 2) % 4
    y_hi = g // 8
    up, down = wrap16(g + 1), wrap16(g - 1)
    sibling = g + 1 - 2 * core
    across = (g + 8) % 16
    greet([(g, wrap16(r + o)) for o in range(1, 16)] + [(wrap16(g + o), r) for o in range(1, 16)])

    def pick(panel, rep):
        return msgs.at[pl.ds(panel * 32 + rep * 2, 2)]

    def ring_copies(o):
        s = wrap16(r + o)
        return (
            remote(pick(0, s), from_next.at[pl.ds(s * 2, 2)], sx.at[0, o], rx.at[0, o], down, r),
            remote(pick(2, s), from_prior.at[pl.ds(s * 2, 2)], sx.at[1, o], rx.at[1, o], up, r),
        )

    def ring_arrivals(o):
        s = wrap16(r + o)
        a = from_next.at[pl.ds(s * 2, 2)]
        b = from_prior.at[pl.ds(s * 2, 2)]
        return (
            remote(a, a, sx.at[0, o], rx.at[0, o], up, r),
            remote(b, b, sx.at[1, o], rx.at[1, o], down, r),
        )

    core_copy = remote(grads.at[:, :, lanes(1 - core, 256)], half_in, s_core, r_core, sibling, r)
    core_copy.start()

    @pl.loop(0, 16)
    def _(i):
        for copy in ring_copies(lax.rem(i + 1, 16)):
            copy.start()

    core_copy.wait_recv()
    for m in range(4):
        half[m] = (grads[m, :, lanes(core, 256)].astype(F32) + half_in[m].astype(F32)).astype(BF)

    def x_row(j):
        return y_hi * 8 + ((x + j) % 4) * 2 + core

    def x_copy(j):
        return remote(half.at[(x + j) % 4], ring_in.at[j - 1], s_ring.at[j], r_ring.at[j], x_row(j), r)

    for j in range(1, 4):
        x_copy(j).start()

    def plane_copy(o):
        s = wrap16(r + o)
        return remote(sums.at[pl.ds(s * 2, 2)], parts.at[pl.ds(r * 2, 2)], sp.at[o], rp.at[o], g, s)

    def plane_arrival(o):
        s = wrap16(r - o)
        view = parts.at[pl.ds(s * 2, 2)]
        return remote(view, view, sp.at[o], rp.at[o], g, s)

    def total(s):
        return (
            msgs[pl.ds(32 + s * 2, 2)].astype(F32)
            + from_next[pl.ds(s * 2, 2)].astype(F32)
            + from_prior[pl.ds(s * 2, 2)].astype(F32)
        ).astype(BF)

    @pl.loop(1, 16)
    def _(o):
        for copy in ring_arrivals(o):
            copy.wait_recv()
        s = wrap16(r + o)
        sums[pl.ds(s * 2, 2)] = total(s)
        plane_copy(o).start()

    for copy in ring_arrivals(0):
        copy.wait_recv()
    parts[pl.ds(r * 2, 2)] = total(r)

    for j in range(1, 4):
        x_copy(j).wait_recv()
    ring[...] = (
        half[x].astype(F32) + ring_in[0].astype(F32) + ring_in[1].astype(F32) + ring_in[2].astype(F32)
    ).astype(BF)
    pair_copy = remote(ring.at[:, lanes(1 - y_hi)], pair_in, s_pair, r_pair, across, r)
    pair_copy.start()
    pair_copy.wait_recv()
    pair[...] = (ring[:, lanes(y_hi)].astype(F32) + pair_in[...].astype(F32)).astype(BF)

    def rep_copy(o):
        s = wrap16(r + o)
        rows = pl.ds(pl.multiple_of(s * 32, 32), 32)
        return remote(pair.at[rows], rep_in.at[o], s_rep.at[o], r_rep.at[o], g, s)

    @pl.loop(1, 16)
    def _(o):
        rep_copy(o).start()

    rep_in[0] = pair[pl.ds(pl.multiple_of(r * 32, 32), 32)]

    @pl.loop(1, 16)
    def _(o):
        plane_arrival(o).wait_recv()

    for f in range(4):
        cut = slice(f * 128, f * 128 + 128)
        value = base[:, :, cut]
        for t in range(4):
            s = (f // 2) * 8 + 2 * t + f % 2
            value = value + parts[2 * s : 2 * s + 2].astype(F32)
        gf[:, :, cut] = value.astype(BF)

    @pl.loop(1, 16)
    def _(o):
        rep_copy(o).wait_recv()

    acc = rep_in[0].astype(F32)
    for o in range(1, 16):
        acc = acc + rep_in[o].astype(F32)
    piece[...] = acc * scale

    def place(row):
        return gout.at[(row // 2) % 4, :, lanes((row % 2) * 2 + row // 8)]

    def row_copy(o):
        return remote(piece, place(g), s_row.at[o], r_row.at[o], wrap16(g + o), r)

    def row_arrival(o):
        src = wrap16(g - o)
        return remote(piece, place(src), s_row.at[o], r_row.at[o], src, r)

    @pl.loop(1, 16)
    def _(o):
        row_copy(o).start()

    gout[x, :, lanes(core * 2 + y_hi)] = piece[...]

    @pl.loop(1, 16)
    def _(o):
        row_arrival(o).wait_recv()

    @pl.loop(0, 16)
    def _(o):
        for copy in ring_copies(o):
            copy.wait_send()

    @pl.loop(1, 16)
    def _(o):
        plane_copy(o).wait_send()
        rep_copy(o).wait_send()
        row_copy(o).wait_send()

    core_copy.wait_send()
    pair_copy.wait_send()
    for j in range(1, 4):
        x_copy(j).wait_send()


def shape(dims, kind):
    return jax.ShapeDtypeStruct(dims, kind)


def local(features, tiles, columns, w_aggregate, w_self, w_middle, w_output, cotangent):
    vmem = pl.BlockSpec(memory_space=VMEM)
    smem = pl.BlockSpec(memory_space=pltpu.SMEM)
    limit = 52 * 1024 * 1024
    feat = features.reshape(2, 128, 512)
    upd, base, tiles_t, cols_t, delt, grads = pl.pallas_call(
        forward_kernel,
        out_shape=(
            shape((256, 512), BF),
            shape((2, 128, 512), F32),
            shape((64, 128, 128), BF),
            shape((4, 2, 8), jnp.int32),
            shape((8, 128, 128), BF),
            shape((4, 512, 512), BF),
        ),
        in_specs=[vmem] * 8,
        out_specs=[vmem] * 6,
        scratch_shapes=[
            VMEM((96, 128, 128), BF),
            pltpu.SMEM((4, 2, 8), jnp.int32),
            VMEM((8, 128, 128), BF),
            VMEM((2, 128, 512), BF),
            VMEM((2, 128, 512), BF),
            VMEM((256, 512), F32),
            VMEM((256, 512), F32),
            DMA((4,)),
            DMA((16,)), DMA((16,)),
            DMA((2, 16)), DMA((2, 16)),
            DMA((4,)), DMA((4,)),
            DMA((4,)), DMA((4,)),
            DMA((4,)), DMA((4,)),
            DMA((4,)), DMA((4,)),
        ],
        compiler_params=pltpu.CompilerParams(
            collective_id=0, has_side_effects=True, vmem_limit_bytes=limit
        ),
        name="forward_pass",
    )(feat, tiles.reshape(16, 128, 128), columns, w_aggregate, w_self, w_middle, w_output, cotangent)
    group = lax.axis_index("row").astype(jnp.int32).reshape(1)
    msgs = pl.pallas_call(
        spread_kernel,
        out_shape=shape((96, 128, 128), BF),
        in_specs=[smem, smem, vmem, vmem],
        out_specs=vmem,
        scratch_shapes=[VMEM((96, 128, 128), F32)],
        compiler_params=pltpu.CompilerParams(vmem_limit_bytes=limit),
        name="spread_messages",
    )(cols_t.reshape(64), group, tiles_t, delt)
    scale = 1.0 / math.sqrt(features.shape[0] * lax.axis_size("row") * lax.axis_size("rep"))
    gf, gout = pl.pallas_call(
        lambda *refs: return_kernel(scale, *refs),
        out_shape=(shape((2, 128, 512), BF), shape((4, 32, 512), F32)),
        in_specs=[vmem] * 3,
        out_specs=[vmem] * 2,
        scratch_shapes=[
            VMEM((32, 128, 128), BF),
            VMEM((32, 128, 128), BF),
            VMEM((32, 128, 128), BF),
            VMEM((32, 128, 128), BF),
            VMEM((4, 512, 256), BF),
            VMEM((4, 512, 256), BF),
            VMEM((3, 512, 256), BF),
            VMEM((512, 256), BF),
            VMEM((512, 128), BF),
            VMEM((512, 128), BF),
            VMEM((16, 32, 128), BF),
            VMEM((32, 128), F32),
            DMA((2, 16)), DMA((2, 16)),
            DMA((16,)), DMA((16,)),
            DMA, DMA,
            DMA((4,)), DMA((4,)),
            DMA, DMA,
            DMA((16,)), DMA((16,)),
            DMA((16,)), DMA((16,)),
        ],
        compiler_params=pltpu.CompilerParams(
            collective_id=1, has_side_effects=True, vmem_limit_bytes=limit
        ),
        name="return_messages",
    )(msgs, base, grads)
    return upd, gf.reshape(256, 512), gout[0], gout[1], gout[2], gout[3]


def solution(mesh):
    placed = (
        P(("row", "rep"), None),
        P(("row", "rep"), None, None, None),
        P(("row", "rep"), None),
        P(),
        P(),
        P(),
        P(),
        P(("row", "rep"), None),
    )
    return jax.shard_map(
        local,
        mesh=mesh,
        in_specs=placed,
        out_specs=(
            P(("row", "rep"), None),
            P(("row", "rep"), None),
            P("rep", None),
            P("rep", None),
            P("rep", None),
            P("rep", None),
        ),
        check_vma=False,
    )
```

```python
import math

import jax
import jax.numpy as jnp
from jax import lax
from jax.experimental import pallas as pl
from jax.experimental.pallas import tpu as pltpu
from jax.sharding import PartitionSpec as P

MESH = pl.DeviceIdType.MESH
BF = jnp.bfloat16
F32 = jnp.float32
VMEM = pltpu.VMEM
DMA = pltpu.SemaphoreType.DMA


def wrap16(value):
    return lax.rem(value + 16, 16)


def quarter(rep):
    return (rep // 8) * 2 + rep % 2


def mate(rep, core, part):
    z = rep % 8
    step = jnp.where((z + core) % 2 == 0, 1, 7)
    other = (z + step) % 8
    return (part // 2) * 8 + jnp.where(z % 2 == part % 2, z, other)


def lanes(part, size=128):
    return pl.ds(pl.multiple_of(part * size, size), size)


def remote(src, dst, send, recv, row, rep):
    return pltpu.make_async_remote_copy(
        src_ref=src, dst_ref=dst, send_sem=send, recv_sem=recv, device_id=(row, rep), device_id_type=MESH
    )


def window_index(column, group):
    panel = jnp.minimum(lax.rem(lax.div(column, 32) - group + 17, 16), 2)
    return panel * 32 + lax.rem(column, 32)


def dot(a, b):
    return jnp.dot(a, b, preferred_element_type=F32)


def dot_bt(a, b):
    return lax.dot_general(a, b, (((1,), (1,)), ((), ())), preferred_element_type=F32)


def dot_at(a, b):
    return lax.dot_general(a, b, (((0,), (0,)), ((), ())), preferred_element_type=F32)


def silu_slope(value):
    sig = jax.nn.sigmoid(value)
    return sig * (1.0 + value * (1.0 - sig))


def greet(peers):
    barrier = pltpu.get_barrier_semaphore()
    for row, rep in peers:
        pl.semaphore_signal(barrier, inc=1, device_id=(row, rep), device_id_type=MESH)
    pl.semaphore_wait(barrier, len(peers))


def layer_kernel(
    scale,
    feat, tiles, cols, w_agg_h, w_self_h, w_mid_h, w_out_h, cot_h,
    upd, gf, gout,
    feat_v, cot_v, w_agg, w_self, w_mid, w_out,
    tiles_t, cols_t, win, cols_s, keys, table, table_s, aggq, aggr, dagg, delt, self_part, cot_part,
    base, grads, csum, to_next, to_prior, from_prior, from_next, sums, parts,
    half_in, half, ring_in, ring, pair_in, pair, rep_in, piece,
    loc, s1, r1, sx, rx, st, rt, sc, rc, sa, ra, sd, rd,
    sm, rm, sp, rp, s_core, r_core, s_ring, r_ring, s_pair, r_pair, s_rep, r_rep, s_row, r_row,
):
    g = lax.axis_index("row")
    r = lax.axis_index("rep")
    core = g % 2
    x = (g // 2) % 4
    y_hi = g // 8
    f = quarter(r)
    up, down = wrap16(g + 1), wrap16(g - 1)
    sibling = g + 1 - 2 * core
    across = (g + 8) % 16

    loads = [
        pltpu.make_async_copy(src, dst, loc.at[i])
        for i, (src, dst) in enumerate(
            (
                (feat, feat_v), (w_self_h, w_self), (cot_h, cot_v), (w_out_h, w_out),
                (w_agg_h, w_agg), (w_mid_h, w_mid),
                (tiles, tiles_t.at[pl.ds(f * 16, 16)]), (cols, cols_t.at[f]),
            )
        )
    ]
    for load in loads:
        load.start()
    greet([(g, wrap16(r + o)) for o in range(1, 16)] + [(wrap16(g + o), r) for o in range(1, 16)])

    def slot(panel, rep):
        return win.at[pl.ds(panel * 32 + rep * 2, 2)]

    def plane_copy(o):
        peer = wrap16(r + o)
        return remote(
            feat.at[:, :, lanes(quarter(peer))], slot(1, r), s1.at[o], r1.at[o], g, peer
        )

    def plane_arrival(o):
        src = wrap16(r - o)
        return remote(slot(1, src), slot(1, src), s1.at[o], r1.at[o], g, src)

    def ring_copies(o):
        src = wrap16(r - o)
        return (
            remote(slot(1, src), slot(0, src), sx.at[0, o], rx.at[0, o], up, r),
            remote(slot(1, src), slot(2, src), sx.at[1, o], rx.at[1, o], down, r),
        )

    def ring_arrivals(o):
        src = wrap16(r - o)
        return (
            remote(slot(0, src), slot(0, src), sx.at[0, o], rx.at[0, o], down, r),
            remote(slot(2, src), slot(2, src), sx.at[1, o], rx.at[1, o], up, r),
        )

    def team(j):
        part = (f + j) % 4
        return part, mate(r, core, part)

    def cols_copy(j):
        return remote(cols, cols_t.at[f], sc.at[j], rc.at[j], g, team(j)[1])

    def cols_arrival(j):
        part, peer = team(4 - j)
        return remote(cols_t.at[part], cols_t.at[part], sc.at[j], rc.at[j], g, peer)

    def tile_copy(j):
        return remote(tiles, tiles_t.at[pl.ds(f * 16, 16)], st.at[j], rt.at[j], g, team(j)[1])

    def tile_arrival(j):
        part, peer = team(4 - j)
        view = tiles_t.at[pl.ds(part * 16, 16)]
        return remote(view, view, st.at[j], rt.at[j], g, peer)

    for j in range(1, 4):
        cols_copy(j).start()

    @pl.loop(1, 16)
    def _(o):
        plane_copy(o).start()

    for j in range(1, 4):
        tile_copy(j).start()

    own = pltpu.make_async_copy(feat.at[:, :, lanes(f)], slot(1, r), loc.at[8])
    own.start()
    own.wait()
    for copy in ring_copies(0):
        copy.start()

    loads[7].wait()
    for j in range(1, 4):
        cols_arrival(j).wait_recv()
    to_smem = pltpu.make_async_copy(cols_t, cols_s, loc.at[9])
    to_smem.start()

    for i in range(4):
        loads[i].wait()
    feat2 = feat_v[...].reshape(256, 512)
    cot2 = cot_v[...]
    self_part[...] = dot(feat2, w_self[...])
    cot_part[...] = dot_bt(cot2, w_out[...])

    @pl.loop(1, 16)
    def _(o):
        plane_arrival(o).wait_recv()
        for copy in ring_copies(o):
            copy.start()

    to_smem.wait()
    lane = lax.broadcasted_iota(jnp.int32, (8, 128), 1)
    start = jnp.zeros((8, 128), jnp.int32)
    slots = []
    for e in range(64):
        index = window_index(cols_s[e // 16, (e // 8) % 2, e % 8], g)
        slots.append(index)
        start = start + (index < lane).astype(jnp.int32)
        keys[e : e + 1, :] = jnp.full((1, 128), index * 64 + e, jnp.int32)
    all_keys = keys[...]
    rank = jnp.zeros((64, 128), jnp.int32)
    for e in range(64):
        rank = rank + (all_keys > slots[e] * 64 + e).astype(jnp.int32)
    lane64 = lax.broadcasted_iota(jnp.int32, (64, 128), 1)
    entry = lax.broadcasted_iota(jnp.int32, (64, 128), 0)
    order = jnp.sum(jnp.where(rank == lane64, entry, 0), axis=0, keepdims=True)
    table[0:8, :] = jnp.broadcast_to(order, (8, 128))
    table[8:16, :] = start
    to_smem = pltpu.make_async_copy(table, table_s, loc.at[10])
    to_smem.start()
    to_smem.wait()

    loads[6].wait()
    for j in range(1, 4):
        tile_arrival(j).wait_recv()

    @pl.loop(0, 16)
    def _(o):
        for copy in ring_arrivals(o):
            copy.wait_recv()

    def agg_copy(j):
        part, peer = team(j)
        return remote(
            aggq.at[pl.ds(part * 2, 2)], aggr.at[:, :, lanes(f)], sa.at[j], ra.at[j], g, peer
        )

    def agg_arrival(j):
        part, peer = team(4 - j)
        view = aggr.at[:, :, lanes(part)]
        return remote(view, view, sa.at[j], ra.at[j], g, peer)

    def block_sum(part, half_of):
        picked = [win[window_index(cols_s[part, half_of, k], g)] for k in range(8)]
        left = jnp.concatenate([tiles_t[part * 16 + half_of * 8 + k] for k in range(8)], axis=1)
        return dot(left, jnp.concatenate(picked, axis=0)).astype(BF)

    for j in (1, 2, 3, 0):
        part = team(j)[0]
        for half_of in range(2):
            summed = block_sum(part, half_of)
            if j:
                aggq[part * 2 + half_of] = summed
            else:
                aggr[half_of, :, lanes(f)] = summed
        if j:
            agg_copy(j).start()
    loads[4].wait()
    loads[5].wait()
    for j in range(1, 4):
        agg_arrival(j).wait_recv()

    agg = aggr[...].reshape(256, 512)
    pre_first = dot(agg, w_agg[...]) + self_part[...]
    first = (pre_first * jax.nn.sigmoid(pre_first)).astype(BF)
    pre_second = dot(first, w_mid[...])
    second = (pre_second * jax.nn.sigmoid(pre_second)).astype(BF)
    delta_second = (cot_part[...] * silu_slope(pre_second)).astype(BF)
    delta_first = (dot_bt(delta_second, w_mid[...]) * silu_slope(pre_first)).astype(BF)
    dagg[...] = dot_bt(delta_first, w_agg[...]).astype(BF).reshape(2, 128, 512)

    def delta_copy(j):
        part, peer = team(j)
        return remote(
            dagg.at[:, :, lanes(part)], delt.at[pl.ds(f * 2, 2)], sd.at[j], rd.at[j], g, peer
        )

    def delta_arrival(j):
        part, peer = team(4 - j)
        view = delt.at[pl.ds(part * 2, 2)]
        return remote(view, view, sd.at[j], rd.at[j], g, peer)

    for j in range(1, 4):
        delta_copy(j).start()
    delt[pl.ds(f * 2, 2)] = dagg[:, :, lanes(f)]
    grads[0] = dot_at(second, cot2).astype(BF)
    grads[1] = dot_at(first, delta_second).astype(BF)
    grads[2] = dot_at(agg, delta_first).astype(BF)
    grads[3] = dot_at(feat2, delta_first).astype(BF)
    core_copy = remote(grads.at[:, :, lanes(1 - core, 256)], half_in, s_core, r_core, sibling, r)
    core_copy.start()
    for j in range(1, 4):
        delta_arrival(j).wait_recv()

    csum[0] = jnp.zeros((128, 128), F32)

    def add_tiles(i, running):
        for step in range(4):
            e = table_s[0, i * 4 + step]
            running = running + dot_at(tiles_t[e], delt[lax.div(e, 8)])
            csum[i * 4 + step + 1] = running
        return running

    lax.fori_loop(0, 16, add_tiles, jnp.zeros((128, 128), F32))

    def message(w):
        return csum[table_s[8, w + 1]] - csum[table_s[8, w]]

    def message_copies(o):
        s = wrap16(r + o)
        rows = pl.ds(s * 2, 2)
        return (
            remote(to_prior.at[rows], from_next.at[rows], sm.at[0, o], rm.at[0, o], down, r),
            remote(to_next.at[rows], from_prior.at[rows], sm.at[1, o], rm.at[1, o], up, r),
        )

    def message_arrivals(o):
        s = wrap16(r + o)
        a = from_next.at[pl.ds(s * 2, 2)]
        b = from_prior.at[pl.ds(s * 2, 2)]
        return (
            remote(a, a, sm.at[0, o], rm.at[0, o], up, r),
            remote(b, b, sm.at[1, o], rm.at[1, o], down, r),
        )

    @pl.loop(0, 16)
    def _(i):
        o = lax.rem(i + 1, 16)
        s = wrap16(r + o)
        for part in range(2):
            to_prior[s * 2 + part] = message(s * 2 + part).astype(BF)
            to_next[s * 2 + part] = message(64 + s * 2 + part).astype(BF)
        for copy in message_copies(o):
            copy.start()

    core_copy.wait_recv()
    for m in range(4):
        half[m] = (grads[m, :, lanes(core, 256)].astype(F32) + half_in[m].astype(F32)).astype(BF)

    def x_row(j):
        return y_hi * 8 + ((x + j) % 4) * 2 + core

    def x_copy(j):
        return remote(half.at[(x + j) % 4], ring_in.at[j - 1], s_ring.at[j], r_ring.at[j], x_row(j), r)

    for j in range(1, 4):
        x_copy(j).start()

    upd[...] = (feat2.astype(F32) + dot(second, w_out[...])).astype(BF)
    base[...] = (cot2.astype(F32) + dot_bt(delta_first, w_self[...])).reshape(2, 128, 512)

    def return_copy(o):
        s = wrap16(r + o)
        return remote(sums.at[pl.ds(s * 2, 2)], parts.at[pl.ds(r * 2, 2)], sp.at[o], rp.at[o], g, s)

    def return_arrival(o):
        s = wrap16(r - o)
        view = parts.at[pl.ds(s * 2, 2)]
        return remote(view, view, sp.at[o], rp.at[o], g, s)

    def total(s, part):
        i = s * 2 + part
        return (message(32 + i) + from_next[i].astype(F32) + from_prior[i].astype(F32)).astype(BF)

    @pl.loop(1, 16)
    def _(o):
        for copy in message_arrivals(o):
            copy.wait_recv()
        s = wrap16(r + o)
        for part in range(2):
            sums[s * 2 + part] = total(s, part)
        return_copy(o).start()

    for copy in message_arrivals(0):
        copy.wait_recv()
    for part in range(2):
        parts[r * 2 + part] = total(r, part)

    for j in range(1, 4):
        x_copy(j).wait_recv()
    ring[...] = (
        half[x].astype(F32) + ring_in[0].astype(F32) + ring_in[1].astype(F32) + ring_in[2].astype(F32)
    ).astype(BF)
    pair_copy = remote(ring.at[:, lanes(1 - y_hi)], pair_in, s_pair, r_pair, across, r)
    pair_copy.start()
    pair_copy.wait_recv()
    pair[...] = (ring[:, lanes(y_hi)].astype(F32) + pair_in[...].astype(F32)).astype(BF)

    def rep_copy(o):
        s = wrap16(r + o)
        rows = pl.ds(pl.multiple_of(s * 32, 32), 32)
        return remote(pair.at[rows], rep_in.at[o], s_rep.at[o], r_rep.at[o], g, s)

    @pl.loop(1, 16)
    def _(o):
        rep_copy(o).start()

    rep_in[0] = pair[pl.ds(pl.multiple_of(r * 32, 32), 32)]

    @pl.loop(1, 16)
    def _(o):
        return_arrival(o).wait_recv()

    for q in range(4):
        cut = slice(q * 128, q * 128 + 128)
        value = base[:, :, cut]
        for t in range(4):
            s = (q // 2) * 8 + 2 * t + q % 2
            value = value + parts[2 * s : 2 * s + 2].astype(F32)
        gf[:, :, cut] = value.astype(BF)

    @pl.loop(1, 16)
    def _(o):
        rep_copy(o).wait_recv()

    acc = rep_in[0].astype(F32)
    for o in range(1, 16):
        acc = acc + rep_in[o].astype(F32)
    piece[...] = acc * scale

    def place(row):
        return gout.at[(row // 2) % 4, :, lanes((row % 2) * 2 + row // 8)]

    def row_copy(o):
        return remote(piece, place(g), s_row.at[o], r_row.at[o], wrap16(g + o), r)

    def row_arrival(o):
        src = wrap16(g - o)
        return remote(piece, place(src), s_row.at[o], r_row.at[o], src, r)

    @pl.loop(1, 16)
    def _(o):
        row_copy(o).start()

    gout[x, :, lanes(core * 2 + y_hi)] = piece[...]

    @pl.loop(1, 16)
    def _(o):
        row_arrival(o).wait_recv()

    @pl.loop(0, 16)
    def _(o):
        for copy in ring_copies(o) + message_copies(o):
            copy.wait_send()

    @pl.loop(1, 16)
    def _(o):
        plane_copy(o).wait_send()
        return_copy(o).wait_send()
        rep_copy(o).wait_send()
        row_copy(o).wait_send()

    core_copy.wait_send()
    pair_copy.wait_send()
    for j in range(1, 4):
        x_copy(j).wait_send()
        cols_copy(j).wait_send()
        tile_copy(j).wait_send()
        agg_copy(j).wait_send()
        delta_copy(j).wait_send()


def shape(dims, kind):
    return jax.ShapeDtypeStruct(dims, kind)


def local(features, tiles, columns, w_aggregate, w_self, w_middle, w_output, cotangent):
    scale = 1.0 / math.sqrt(features.shape[0] * lax.axis_size("row") * lax.axis_size("rep"))
    weight = VMEM((512, 512), BF)
    panel = VMEM((32, 128, 128), BF)
    upd, gf, gout = pl.pallas_call(
        lambda *refs: layer_kernel(scale, *refs),
        out_shape=(shape((256, 512), BF), shape((2, 128, 512), BF), shape((4, 32, 512), F32)),
        in_specs=[pl.BlockSpec(memory_space=pl.ANY)] * 8,
        out_specs=[pl.BlockSpec(memory_space=VMEM)] * 3,
        scratch_shapes=[
            VMEM((2, 128, 512), BF), VMEM((256, 512), BF), weight, weight, weight, weight,
            VMEM((64, 128, 128), BF), VMEM((4, 2, 8), jnp.int32), VMEM((96, 128, 128), BF),
            pltpu.SMEM((4, 2, 8), jnp.int32), VMEM((64, 128), jnp.int32),
            VMEM((16, 128), jnp.int32), pltpu.SMEM((16, 128), jnp.int32),
            VMEM((8, 128, 128), BF), VMEM((2, 128, 512), BF), VMEM((2, 128, 512), BF),
            VMEM((8, 128, 128), BF), VMEM((256, 512), F32), VMEM((256, 512), F32),
            VMEM((2, 128, 512), F32), VMEM((4, 512, 512), BF), VMEM((65, 128, 128), F32),
            panel, panel, panel, panel, panel, panel,
            VMEM((4, 512, 256), BF), VMEM((4, 512, 256), BF), VMEM((3, 512, 256), BF), VMEM((512, 256), BF),
            VMEM((512, 128), BF), VMEM((512, 128), BF), VMEM((16, 32, 128), BF), VMEM((32, 128), F32),
            DMA((11,)),
            DMA((16,)), DMA((16,)),
            DMA((2, 16)), DMA((2, 16)),
            DMA((4,)), DMA((4,)),
            DMA((4,)), DMA((4,)),
            DMA((4,)), DMA((4,)),
            DMA((4,)), DMA((4,)),
            DMA((2, 16)), DMA((2, 16)),
            DMA((16,)), DMA((16,)),
            DMA, DMA,
            DMA((4,)), DMA((4,)),
            DMA, DMA,
            DMA((16,)), DMA((16,)),
            DMA((16,)), DMA((16,)),
        ],
        compiler_params=pltpu.CompilerParams(
            collective_id=0, has_side_effects=True, vmem_limit_bytes=60 * 1024 * 1024
        ),
        name="message_passing_layer",
    )(
        features.reshape(2, 128, 512), tiles.reshape(16, 128, 128), columns,
        w_aggregate, w_self, w_middle, w_output, cotangent,
    )
    return upd, gf.reshape(256, 512), gout[0], gout[1], gout[2], gout[3]


def solution(mesh):
    placed = (
        P(("row", "rep"), None),
        P(("row", "rep"), None, None, None),
        P(("row", "rep"), None),
        P(),
        P(),
        P(),
        P(),
        P(("row", "rep"), None),
    )
    return jax.shard_map(
        local,
        mesh=mesh,
        in_specs=placed,
        out_specs=(
            P(("row", "rep"), None),
            P(("row", "rep"), None),
            P("rep", None),
            P("rep", None),
            P("rep", None),
            P("rep", None),
        ),
        check_vma=False,
    )
```

```python
import math

import jax
import jax.numpy as jnp
from jax import lax
from jax.experimental import pallas as pl
from jax.experimental.pallas import tpu as pltpu
from jax.sharding import PartitionSpec as P

MESH = pl.DeviceIdType.MESH
BF = jnp.bfloat16
F32 = jnp.float32
VMEM = pltpu.VMEM
DMA = pltpu.SemaphoreType.DMA
HANDED_ALONG_Z = 2


def wrap16(value):
    return lax.rem(value + 16, 16)


def quarter(rep):
    return (rep // 8) * 2 + rep % 2


def mate(rep, core, part):
    z = rep % 8
    step = jnp.where((z + core) % 2 == 0, 1, 7)
    other = (z + step) % 8
    return (part // 2) * 8 + jnp.where(z % 2 == part % 2, z, other)


def lanes(part, size=128):
    return pl.ds(pl.multiple_of(part * size, size), size)


def remote(src, dst, send, recv, row, rep):
    return pltpu.make_async_remote_copy(
        src_ref=src, dst_ref=dst, send_sem=send, recv_sem=recv, device_id=(row, rep), device_id_type=MESH
    )


def window_index(column, group):
    panel = jnp.minimum(lax.rem(lax.div(column, 32) - group + 17, 16), 2)
    return panel * 32 + lax.rem(column, 32)


def dot(a, b):
    return jnp.dot(a, b, preferred_element_type=F32)


def dot_bt(a, b):
    return lax.dot_general(a, b, (((1,), (1,)), ((), ())), preferred_element_type=F32)


def dot_at(a, b):
    return lax.dot_general(a, b, (((0,), (0,)), ((), ())), preferred_element_type=F32)


def silu_slope(value):
    sig = jax.nn.sigmoid(value)
    return sig * (1.0 + value * (1.0 - sig))


def greet(peers):
    barrier = pltpu.get_barrier_semaphore()
    for row, rep in peers:
        pl.semaphore_signal(barrier, inc=1, device_id=(row, rep), device_id_type=MESH)
    pl.semaphore_wait(barrier, len(peers))


def layer_kernel(
    scale,
    feat, tiles, cols, w_agg_h, w_self_h, w_mid_h, w_out_h, cot_h,
    upd, gf, gout,
    feat_v, cot_v, w_agg, w_self, w_mid, w_out,
    tiles_t, cols_t, win, cols_s, keys, table, table_s, aggq, aggr, dagg, delt, self_part, cot_part,
    base, grads, csum, to_next, to_prior, from_prior, from_next, sums, parts,
    half_in, half, ring_in, ring, pair_in, pair, rep_in, piece,
    from_mate, loc, s_mate, r_mate, s1, r1, sx, rx, st, rt, sc, rc, sa, ra, sd, rd,
    sm, rm, sp, rp, s_core, r_core, s_ring, r_ring, s_pair, r_pair, s_rep, r_rep, s_row, r_row,
):
    g = lax.axis_index("row")
    r = lax.axis_index("rep")
    core = g % 2
    x = (g // 2) % 4
    y_hi = g // 8
    f = quarter(r)
    up, down = wrap16(g + 1), wrap16(g - 1)
    sibling = g + 1 - 2 * core
    across = (g + 8) % 16
    y, z = r // 8, r % 8
    y_mate = (1 - y) * 8 + z
    z_mate = y * 8 + (z + jnp.where((z + core) % 2 == 0, 1, 7)) % 8

    loads = [
        pltpu.make_async_copy(src, dst, loc.at[i])
        for i, (src, dst) in enumerate(
            (
                (feat, feat_v), (w_self_h, w_self), (cot_h, cot_v), (w_out_h, w_out),
                (w_agg_h, w_agg), (w_mid_h, w_mid),
                (tiles, tiles_t.at[pl.ds(f * 16, 16)]), (cols, cols_t.at[f]),
            )
        )
    ]
    for load in loads:
        load.start()
    greet([(g, wrap16(r + o)) for o in range(1, 16)] + [(wrap16(g + o), r) for o in range(1, 16)] + [(across, y_mate)])

    def slot(panel, rep):
        return win.at[pl.ds(panel * 32 + rep * 2, 2)]

    def source(row, d):
        return jnp.where(row == 0, y, 1 - y) * 8 + (z - d + 8) % 8

    def mate_copy():
        return remote(feat.at[:, :, lanes(1 - y, 256)], from_mate, s_mate, r_mate, g, y_mate)

    def chunk_copy(row, d, held=0):
        peer = y * 8 + (z - held + d) % 8
        if held:
            src = slot(1, source(row, held))
        else:
            src = (feat, from_mate)[row].at[:, :, lanes(quarter(peer) if row == 0 else peer % 2)]
        dst = slot(1, source(row, held))
        return remote(src, dst, s1.at[row, d], r1.at[row, d], g, peer)

    def chunk_arrival(row, d):
        view = slot(1, source(row, d))
        return remote(view, view, s1.at[row, d], r1.at[row, d], g, y * 8 + (z - d + 8) % 8)

    def ring_copies(row, d):
        src = source(row, d)
        return (
            remote(slot(1, src), slot(0, src), sx.at[row, d, 0], rx.at[row, d, 0], up, r),
            remote(slot(1, src), slot(2, src), sx.at[row, d, 1], rx.at[row, d, 1], down, r),
        )

    def ring_arrivals(row, d):
        src = source(row, d)
        return (
            remote(slot(0, src), slot(0, src), sx.at[row, d, 0], rx.at[row, d, 0], down, r),
            remote(slot(2, src), slot(2, src), sx.at[row, d, 1], rx.at[row, d, 1], up, r),
        )

    def send_ring(row, d):
        for copy in ring_copies(row, d):
            copy.start()

    def pass_on(row, d):
        chunk_arrival(row, d).wait_recv()
        if d in (1, 7):
            chunk_copy(row, 3 if d == 1 else 5, held=d).start()
        if d == (2 if row == 0 else 6):
            chunk_copy(row, 4, held=d).start()
        send_ring(row, d)

    def team(j):
        part = (f + j) % 4
        return part, mate(r, core, part)

    def cols_copy(j):
        return remote(cols, cols_t.at[f], sc.at[j], rc.at[j], g, team(j)[1])

    def cols_arrival(j):
        part, peer = team(4 - j)
        return remote(cols_t.at[part], cols_t.at[part], sc.at[j], rc.at[j], g, peer)

    def piece_of(rep, i):
        return tiles_t.at[pl.ds(quarter(rep) * 16 + i * 4, 4)]

    def tile_copy(way, i):
        peer = (y_mate, z_mate)[way]
        return remote(tiles.at[pl.ds(i * 4, 4)], piece_of(r, i), st.at[way, i], rt.at[way, i], g, peer)

    def tile_arrival(way, i):
        peer = (y_mate, z_mate)[way]
        return remote(piece_of(peer, i), piece_of(peer, i), st.at[way, i], rt.at[way, i], g, peer)

    def hand_copy(i):
        src, peer = (y_mate, z_mate) if i < HANDED_ALONG_Z else (z_mate, y_mate)
        return remote(piece_of(src, i), piece_of(src, i), st.at[2, i], rt.at[2, i], g, peer)

    def hand_arrival(i):
        far = mate(r, core, 3 - f)
        peer = z_mate if i < HANDED_ALONG_Z else y_mate
        return remote(piece_of(far, i), piece_of(far, i), st.at[2, i], rt.at[2, i], g, peer)

    for j in range(1, 4):
        cols_copy(j).start()

    mate_copy().start()
    for d in (1, 7, 2, 6):
        chunk_copy(0, d).start()
    for i in range(4):
        tile_copy(0, i).start()
    for i in range(HANDED_ALONG_Z, 4):
        tile_copy(1, i).start()
    own = pltpu.make_async_copy(feat.at[:, :, lanes(f)], slot(1, r), loc.at[8])
    own.start()
    own.wait()
    send_ring(0, 0)
    mate_copy().wait_recv()
    for d in (1, 7, 2, 6):
        chunk_copy(1, d).start()
    for i in range(HANDED_ALONG_Z):
        tile_copy(1, i).start()
    own = pltpu.make_async_copy(from_mate.at[:, :, lanes(z % 2)], slot(1, y_mate), loc.at[11])
    own.start()
    own.wait()
    send_ring(1, 0)
    for d in (1, 7, 2, 6):
        pass_on(0, d)
    for i in range(HANDED_ALONG_Z):
        tile_arrival(0, i).wait_recv()
        hand_copy(i).start()

    loads[7].wait()
    for j in range(1, 4):
        cols_arrival(j).wait_recv()
    to_smem = pltpu.make_async_copy(cols_t, cols_s, loc.at[9])
    to_smem.start()

    for i in range(4):
        loads[i].wait()
    feat2 = feat_v[...].reshape(256, 512)
    cot2 = cot_v[...]
    self_part[...] = dot(feat2, w_self[...])
    cot_part[...] = dot_bt(cot2, w_out[...])

    for d in (1, 7, 2, 6):
        pass_on(1, d)
    for i in range(HANDED_ALONG_Z, 4):
        tile_arrival(1, i).wait_recv()
        hand_copy(i).start()

    to_smem.wait()
    lane = lax.broadcasted_iota(jnp.int32, (8, 128), 1)
    start = jnp.zeros((8, 128), jnp.int32)
    slots = []
    for e in range(64):
        index = window_index(cols_s[e // 16, (e // 8) % 2, e % 8], g)
        slots.append(index)
        start = start + (index < lane).astype(jnp.int32)
        keys[e : e + 1, :] = jnp.full((1, 128), index * 64 + e, jnp.int32)
    all_keys = keys[...]
    rank = jnp.zeros((64, 128), jnp.int32)
    for e in range(64):
        rank = rank + (all_keys > slots[e] * 64 + e).astype(jnp.int32)
    lane64 = lax.broadcasted_iota(jnp.int32, (64, 128), 1)
    entry = lax.broadcasted_iota(jnp.int32, (64, 128), 0)
    order = jnp.sum(jnp.where(rank == lane64, entry, 0), axis=0, keepdims=True)
    table[0:8, :] = jnp.broadcast_to(order, (8, 128))
    table[8:16, :] = start
    to_smem = pltpu.make_async_copy(table, table_s, loc.at[10])
    to_smem.start()
    to_smem.wait()

    for d in (3, 5, 4):
        for row in range(2):
            pass_on(row, d)
    loads[6].wait()
    for i in range(HANDED_ALONG_Z, 4):
        tile_arrival(0, i).wait_recv()
    for i in range(HANDED_ALONG_Z):
        tile_arrival(1, i).wait_recv()
    for i in range(4):
        hand_arrival(i).wait_recv()
    for d in range(8):
        for row in range(2):
            for copy in ring_arrivals(row, d):
                copy.wait_recv()

    def agg_copy(j):
        part, peer = team(j)
        return remote(
            aggq.at[pl.ds(part * 2, 2)], aggr.at[:, :, lanes(f)], sa.at[j], ra.at[j], g, peer
        )

    def agg_arrival(j):
        part, peer = team(4 - j)
        view = aggr.at[:, :, lanes(part)]
        return remote(view, view, sa.at[j], ra.at[j], g, peer)

    def block_sum(part, half_of):
        picked = [win[window_index(cols_s[part, half_of, k], g)] for k in range(8)]
        left = jnp.concatenate([tiles_t[part * 16 + half_of * 8 + k] for k in range(8)], axis=1)
        return dot(left, jnp.concatenate(picked, axis=0)).astype(BF)

    for j in (1, 2, 3, 0):
        part = team(j)[0]
        for half_of in range(2):
            summed = block_sum(part, half_of)
            if j:
                aggq[part * 2 + half_of] = summed
            else:
                aggr[half_of, :, lanes(f)] = summed
        if j:
            agg_copy(j).start()
    loads[4].wait()
    loads[5].wait()
    for j in range(1, 4):
        agg_arrival(j).wait_recv()

    agg = aggr[...].reshape(256, 512)
    pre_first = dot(agg, w_agg[...]) + self_part[...]
    first = (pre_first * jax.nn.sigmoid(pre_first)).astype(BF)
    pre_second = dot(first, w_mid[...])
    second = (pre_second * jax.nn.sigmoid(pre_second)).astype(BF)
    delta_second = (cot_part[...] * silu_slope(pre_second)).astype(BF)
    delta_first = (dot_bt(delta_second, w_mid[...]) * silu_slope(pre_first)).astype(BF)
    dagg[...] = dot_bt(delta_first, w_agg[...]).astype(BF).reshape(2, 128, 512)

    def delta_copy(j):
        part, peer = team(j)
        return remote(
            dagg.at[:, :, lanes(part)], delt.at[pl.ds(f * 2, 2)], sd.at[j], rd.at[j], g, peer
        )

    def delta_arrival(j):
        part, peer = team(4 - j)
        view = delt.at[pl.ds(part * 2, 2)]
        return remote(view, view, sd.at[j], rd.at[j], g, peer)

    for j in range(1, 4):
        delta_copy(j).start()
    delt[pl.ds(f * 2, 2)] = dagg[:, :, lanes(f)]
    grads[0] = dot_at(second, cot2).astype(BF)
    grads[1] = dot_at(first, delta_second).astype(BF)
    grads[2] = dot_at(agg, delta_first).astype(BF)
    grads[3] = dot_at(feat2, delta_first).astype(BF)
    core_copy = remote(grads.at[:, :, lanes(1 - core, 256)], half_in, s_core, r_core, sibling, r)
    core_copy.start()
    for j in range(1, 4):
        delta_arrival(j).wait_recv()

    csum[0] = jnp.zeros((128, 128), F32)

    def add_tiles(i, running):
        for step in range(4):
            e = table_s[0, i * 4 + step]
            running = running + dot_at(tiles_t[e], delt[lax.div(e, 8)])
            csum[i * 4 + step + 1] = running
        return running

    lax.fori_loop(0, 16, add_tiles, jnp.zeros((128, 128), F32))

    def message(w):
        return csum[table_s[8, w + 1]] - csum[table_s[8, w]]

    def message_copies(o):
        s = wrap16(r + o)
        rows = pl.ds(s * 2, 2)
        return (
            remote(to_prior.at[rows], from_next.at[rows], sm.at[0, o], rm.at[0, o], down, r),
            remote(to_next.at[rows], from_prior.at[rows], sm.at[1, o], rm.at[1, o], up, r),
        )

    def message_arrivals(o):
        s = wrap16(r + o)
        a = from_next.at[pl.ds(s * 2, 2)]
        b = from_prior.at[pl.ds(s * 2, 2)]
        return (
            remote(a, a, sm.at[0, o], rm.at[0, o], up, r),
            remote(b, b, sm.at[1, o], rm.at[1, o], down, r),
        )

    @pl.loop(0, 16)
    def _(i):
        o = lax.rem(i + 1, 16)
        s = wrap16(r + o)
        for part in range(2):
            to_prior[s * 2 + part] = message(s * 2 + part).astype(BF)
            to_next[s * 2 + part] = message(64 + s * 2 + part).astype(BF)
        for copy in message_copies(o):
            copy.start()

    core_copy.wait_recv()
    for m in range(4):
        half[m] = (grads[m, :, lanes(core, 256)].astype(F32) + half_in[m].astype(F32)).astype(BF)

    def y_copy(j):
        row, rep = across if j & 2 else g, y_mate if j & 1 else r
        rows = pl.ds(pl.multiple_of((rep // 8) * 256, 256), 256)
        return remote(half.at[:, rows, lanes(row // 8)], pair_in.at[j - 1], s_pair.at[j], r_pair.at[j], row, rep)

    for j in range(1, 4):
        y_copy(j).start()

    upd[...] = (feat2.astype(F32) + dot(second, w_out[...])).astype(BF)
    base[...] = (cot2.astype(F32) + dot_bt(delta_first, w_self[...])).reshape(2, 128, 512)

    def return_copy(o):
        s = wrap16(r + o)
        return remote(sums.at[pl.ds(s * 2, 2)], parts.at[pl.ds(r * 2, 2)], sp.at[o], rp.at[o], g, s)

    def return_arrival(o):
        s = wrap16(r - o)
        view = parts.at[pl.ds(s * 2, 2)]
        return remote(view, view, sp.at[o], rp.at[o], g, s)

    def total(s, part):
        i = s * 2 + part
        return (message(32 + i) + from_next[i].astype(F32) + from_prior[i].astype(F32)).astype(BF)

    @pl.loop(1, 16)
    def _(o):
        for copy in message_arrivals(o):
            copy.wait_recv()
        s = wrap16(r + o)
        for part in range(2):
            sums[s * 2 + part] = total(s, part)
        return_copy(o).start()

    for copy in message_arrivals(0):
        copy.wait_recv()
    for part in range(2):
        parts[r * 2 + part] = total(r, part)

    for j in range(1, 4):
        y_copy(j).wait_recv()
    own_rows = pl.ds(pl.multiple_of(y * 256, 256), 256)
    for m in range(4):
        value = half[m, own_rows, lanes(y_hi)].astype(F32)
        for j in range(3):
            value = value + pair_in[j, m].astype(F32)
        pair[m] = value.astype(BF)

    def x_row(j):
        return y_hi * 8 + ((x + j) % 4) * 2 + core

    def x_copy(j):
        return remote(pair.at[(x + j) % 4], ring_in.at[j - 1], s_ring.at[j], r_ring.at[j], x_row(j), r)

    for j in range(1, 4):
        x_copy(j).start()
    for j in range(1, 4):
        x_copy(j).wait_recv()
    ring[...] = (
        pair[x].astype(F32) + ring_in[0].astype(F32) + ring_in[1].astype(F32) + ring_in[2].astype(F32)
    ).astype(BF)

    def rep_copy(d):
        to = (z + d) % 8
        rows = pl.ds(pl.multiple_of(to * 32, 32), 32)
        return remote(ring.at[rows], rep_in.at[d], s_rep.at[d], r_rep.at[d], g, y * 8 + to)

    for d in range(1, 8):
        rep_copy(d).start()
    acc = ring[pl.ds(pl.multiple_of(z * 32, 32), 32)].astype(F32)
    for d in range(1, 8):
        rep_copy(d).wait_recv()
        acc = acc + rep_in[d].astype(F32)
    piece[...] = acc * scale

    def place(row):
        return gout.at[(row // 2) % 4, :, lanes((row % 2) * 2 + row // 8)]

    def row_copy(o):
        return remote(piece, place(g), s_row.at[o], r_row.at[o], wrap16(g + o), r)

    def row_arrival(o):
        src = wrap16(g - o)
        return remote(piece, place(src), s_row.at[o], r_row.at[o], src, r)

    @pl.loop(1, 16)
    def _(o):
        row_copy(o).start()

    gout[x, :, lanes(core * 2 + y_hi)] = piece[...]

    @pl.loop(1, 16)
    def _(o):
        return_arrival(o).wait_recv()

    for q in range(4):
        cut = slice(q * 128, q * 128 + 128)
        value = base[:, :, cut]
        for t in range(4):
            s = (q // 2) * 8 + 2 * t + q % 2
            value = value + parts[2 * s : 2 * s + 2].astype(F32)
        gf[:, :, cut] = value.astype(BF)

    @pl.loop(1, 16)
    def _(o):
        row_arrival(o).wait_recv()

    @pl.loop(0, 16)
    def _(o):
        for copy in message_copies(o):
            copy.wait_send()

    @pl.loop(1, 16)
    def _(o):
        return_copy(o).wait_send()
        row_copy(o).wait_send()

    mate_copy().wait_send()
    for row in range(2):
        for d in (1, 7, 2, 6):
            chunk_copy(row, d).wait_send()
        chunk_copy(row, 3, held=1).wait_send()
        chunk_copy(row, 5, held=7).wait_send()
        chunk_copy(row, 4, held=2 if row == 0 else 6).wait_send()
        for d in range(8):
            for copy in ring_copies(row, d):
                copy.wait_send()
    for i in range(4):
        tile_copy(0, i).wait_send()
        tile_copy(1, i).wait_send()
        hand_copy(i).wait_send()
    core_copy.wait_send()
    for j in range(1, 4):
        y_copy(j).wait_send()
        x_copy(j).wait_send()
        cols_copy(j).wait_send()
        agg_copy(j).wait_send()
        delta_copy(j).wait_send()
    for d in range(1, 8):
        rep_copy(d).wait_send()


def shape(dims, kind):
    return jax.ShapeDtypeStruct(dims, kind)


def local(features, tiles, columns, w_aggregate, w_self, w_middle, w_output, cotangent):
    scale = 1.0 / math.sqrt(features.shape[0] * lax.axis_size("row") * lax.axis_size("rep"))
    weight = VMEM((512, 512), BF)
    panel = VMEM((32, 128, 128), BF)
    upd, gf, gout = pl.pallas_call(
        lambda *refs: layer_kernel(scale, *refs),
        out_shape=(shape((256, 512), BF), shape((2, 128, 512), BF), shape((4, 32, 512), F32)),
        in_specs=[pl.BlockSpec(memory_space=pltpu.HBM)] * 8,
        out_specs=[pl.BlockSpec(memory_space=VMEM)] * 3,
        scratch_shapes=[
            VMEM((2, 128, 512), BF), VMEM((256, 512), BF), weight, weight, weight, weight,
            VMEM((64, 128, 128), BF), VMEM((4, 2, 8), jnp.int32), VMEM((96, 128, 128), BF),
            pltpu.SMEM((4, 2, 8), jnp.int32), VMEM((64, 128), jnp.int32),
            VMEM((16, 128), jnp.int32), pltpu.SMEM((16, 128), jnp.int32),
            VMEM((8, 128, 128), BF), VMEM((2, 128, 512), BF), VMEM((2, 128, 512), BF),
            VMEM((8, 128, 128), BF), VMEM((256, 512), F32), VMEM((256, 512), F32),
            VMEM((2, 128, 512), F32), VMEM((4, 512, 512), BF), VMEM((65, 128, 128), F32),
            panel, panel, panel, panel, panel, panel,
            VMEM((4, 512, 256), BF), VMEM((4, 512, 256), BF), VMEM((3, 256, 128), BF), VMEM((256, 128), BF),
            VMEM((3, 4, 256, 128), BF), VMEM((4, 256, 128), BF), VMEM((8, 32, 128), BF), VMEM((32, 128), F32),
            VMEM((2, 128, 256), BF),
            DMA((12,)), DMA, DMA,
            DMA((2, 8)), DMA((2, 8)),
            DMA((2, 8, 2)), DMA((2, 8, 2)),
            DMA((3, 4)), DMA((3, 4)),
            DMA((4,)), DMA((4,)),
            DMA((4,)), DMA((4,)),
            DMA((4,)), DMA((4,)),
            DMA((2, 16)), DMA((2, 16)),
            DMA((16,)), DMA((16,)),
            DMA, DMA,
            DMA((4,)), DMA((4,)),
            DMA((4,)), DMA((4,)),
            DMA((8,)), DMA((8,)),
            DMA((16,)), DMA((16,)),
        ],
        compiler_params=pltpu.CompilerParams(
            collective_id=0, has_side_effects=True, vmem_limit_bytes=52 * 1024 * 1024
        ),
        name="message_passing_layer",
    )(
        features.reshape(2, 128, 512), tiles.reshape(16, 128, 128), columns,
        w_aggregate, w_self, w_middle, w_output, cotangent,
    )
    return upd, gf.reshape(256, 512), gout[0], gout[1], gout[2], gout[3]


def solution(mesh):
    placed = (
        P(("row", "rep"), None),
        P(("row", "rep"), None, None, None),
        P(("row", "rep"), None),
        P(),
        P(),
        P(),
        P(),
        P(("row", "rep"), None),
    )
    return jax.shard_map(
        local,
        mesh=mesh,
        in_specs=placed,
        out_specs=(
            P(("row", "rep"), None),
            P(("row", "rep"), None),
            P("rep", None),
            P("rep", None),
            P("rep", None),
            P("rep", None),
        ),
        check_vma=False,
    )
```

```python
import math

import jax
import jax.numpy as jnp
from jax import lax
from jax.experimental import pallas as pl
from jax.experimental.pallas import tpu as pltpu
from jax.sharding import PartitionSpec as P

MESH = pl.DeviceIdType.MESH
BF = jnp.bfloat16
F32 = jnp.float32
VMEM = pltpu.VMEM
DMA = pltpu.SemaphoreType.DMA
HANDED_ALONG_Z = 2
Y_SUM_AT, X_SUM_AT = 8, 12


def wrap16(value):
    return lax.rem(value + 16, 16)


def quarter(rep):
    return (rep // 8) * 2 + rep % 2


def mate(rep, core, part):
    z = rep % 8
    step = jnp.where((z + core) % 2 == 0, 1, 7)
    other = (z + step) % 8
    return (part // 2) * 8 + jnp.where(z % 2 == part % 2, z, other)


def lanes(part, size=128):
    return pl.ds(pl.multiple_of(part * size, size), size)


def remote(src, dst, send, recv, row, rep):
    return pltpu.make_async_remote_copy(
        src_ref=src, dst_ref=dst, send_sem=send, recv_sem=recv, device_id=(row, rep), device_id_type=MESH
    )


def window_index(column, group):
    panel = jnp.minimum(lax.rem(lax.div(column, 32) - group + 17, 16), 2)
    return panel * 32 + lax.rem(column, 32)


def dot(a, b):
    return jnp.dot(a, b, preferred_element_type=F32)


def dot_bt(a, b):
    return lax.dot_general(a, b, (((1,), (1,)), ((), ())), preferred_element_type=F32)


def dot_at(a, b):
    return lax.dot_general(a, b, (((0,), (0,)), ((), ())), preferred_element_type=F32)


def silu_slope(value):
    sig = jax.nn.sigmoid(value)
    return sig * (1.0 + value * (1.0 - sig))


def greet(peers):
    barrier = pltpu.get_barrier_semaphore()
    for row, rep in peers:
        pl.semaphore_signal(barrier, inc=1, device_id=(row, rep), device_id_type=MESH)
    pl.semaphore_wait(barrier, len(peers))


def layer_kernel(
    scale,
    feat, tiles, cols, w_agg_h, w_self_h, w_mid_h, w_out_h, cot_h,
    upd, gf, gout,
    feat_v, cot_v, w_agg, w_self, w_mid, w_out,
    tiles_t, cols_t, win, cols_s, keys, table, table_s, aggq, aggr, dagg, delt, self_part, cot_part,
    base, grads, csum, to_next, to_prior, from_prior, from_next, sums, parts,
    half_in, half, ring_in, ring, pair_in, pair, rep_in, piece,
    from_mate, loc, s_mate, r_mate, s1, r1, sx, rx, st, rt, sc, rc, sa, ra, sd, rd,
    sm, rm, sp, rp, s_core, r_core, s_ring, r_ring, s_pair, r_pair, s_rep, r_rep, s_row, r_row,
):
    g = lax.axis_index("row")
    r = lax.axis_index("rep")
    core = g % 2
    x = (g // 2) % 4
    y_hi = g // 8
    f = quarter(r)
    up, down = wrap16(g + 1), wrap16(g - 1)
    sibling = g + 1 - 2 * core
    across = (g + 8) % 16
    y, z = r // 8, r % 8
    y_mate = (1 - y) * 8 + z
    z_mate = y * 8 + (z + jnp.where((z + core) % 2 == 0, 1, 7)) % 8

    loads = [
        pltpu.make_async_copy(src, dst, loc.at[i])
        for i, (src, dst) in enumerate(
            (
                (feat, feat_v), (w_self_h, w_self), (cot_h, cot_v), (w_out_h, w_out),
                (w_agg_h, w_agg), (w_mid_h, w_mid),
                (tiles, tiles_t.at[pl.ds(f * 16, 16)]), (cols, cols_t.at[f]),
            )
        )
    ]
    for load in loads:
        load.start()
    greet([(g, wrap16(r + o)) for o in range(1, 16)] + [(wrap16(g + o), r) for o in range(1, 16)] + [(across, y_mate)])

    def slot(panel, rep):
        return win.at[pl.ds(panel * 32 + rep * 2, 2)]

    def source(row, d):
        return jnp.where(row == 0, y, 1 - y) * 8 + (z - d + 8) % 8

    def mate_copy():
        return remote(feat.at[:, :, lanes(1 - y, 256)], from_mate, s_mate, r_mate, g, y_mate)

    def chunk_copy(row, d, held=0):
        peer = y * 8 + (z - held + d) % 8
        if held:
            src = slot(1, source(row, held))
        else:
            src = (feat, from_mate)[row].at[:, :, lanes(quarter(peer) if row == 0 else peer % 2)]
        dst = slot(1, source(row, held))
        return remote(src, dst, s1.at[row, d], r1.at[row, d], g, peer)

    def chunk_arrival(row, d):
        view = slot(1, source(row, d))
        return remote(view, view, s1.at[row, d], r1.at[row, d], g, y * 8 + (z - d + 8) % 8)

    def ring_copies(row, d):
        src = source(row, d)
        return (
            remote(slot(1, src), slot(0, src), sx.at[row, d, 0], rx.at[row, d, 0], up, r),
            remote(slot(1, src), slot(2, src), sx.at[row, d, 1], rx.at[row, d, 1], down, r),
        )

    def ring_arrivals(row, d):
        src = source(row, d)
        return (
            remote(slot(0, src), slot(0, src), sx.at[row, d, 0], rx.at[row, d, 0], down, r),
            remote(slot(2, src), slot(2, src), sx.at[row, d, 1], rx.at[row, d, 1], up, r),
        )

    def send_ring(row, d):
        for copy in ring_copies(row, d):
            copy.start()

    def pass_on(row, d):
        chunk_arrival(row, d).wait_recv()
        if d in (1, 7):
            chunk_copy(row, 3 if d == 1 else 5, held=d).start()
        if d == (2 if row == 0 else 6):
            chunk_copy(row, 4, held=d).start()
        send_ring(row, d)

    def team(j):
        part = (f + j) % 4
        return part, mate(r, core, part)

    def cols_copy(j):
        return remote(cols, cols_t.at[f], sc.at[j], rc.at[j], g, team(j)[1])

    def cols_arrival(j):
        part, peer = team(4 - j)
        return remote(cols_t.at[part], cols_t.at[part], sc.at[j], rc.at[j], g, peer)

    def piece_of(rep, i):
        return tiles_t.at[pl.ds(quarter(rep) * 16 + i * 4, 4)]

    def tile_copy(way, i):
        peer = (y_mate, z_mate)[way]
        return remote(tiles.at[pl.ds(i * 4, 4)], piece_of(r, i), st.at[way, i], rt.at[way, i], g, peer)

    def tile_arrival(way, i):
        peer = (y_mate, z_mate)[way]
        return remote(piece_of(peer, i), piece_of(peer, i), st.at[way, i], rt.at[way, i], g, peer)

    def hand_copy(i):
        src, peer = (y_mate, z_mate) if i < HANDED_ALONG_Z else (z_mate, y_mate)
        return remote(piece_of(src, i), piece_of(src, i), st.at[2, i], rt.at[2, i], g, peer)

    def hand_arrival(i):
        far = mate(r, core, 3 - f)
        peer = z_mate if i < HANDED_ALONG_Z else y_mate
        return remote(piece_of(far, i), piece_of(far, i), st.at[2, i], rt.at[2, i], g, peer)

    for j in range(1, 4):
        cols_copy(j).start()

    mate_copy().start()
    for d in (1, 7, 2, 6):
        chunk_copy(0, d).start()
    for i in range(4):
        tile_copy(0, i).start()
    for i in range(HANDED_ALONG_Z, 4):
        tile_copy(1, i).start()
    own = pltpu.make_async_copy(feat.at[:, :, lanes(f)], slot(1, r), loc.at[8])
    own.start()
    own.wait()
    send_ring(0, 0)
    mate_copy().wait_recv()
    for d in (1, 7, 2, 6):
        chunk_copy(1, d).start()
    for i in range(HANDED_ALONG_Z):
        tile_copy(1, i).start()
    own = pltpu.make_async_copy(from_mate.at[:, :, lanes(z % 2)], slot(1, y_mate), loc.at[11])
    own.start()
    own.wait()
    send_ring(1, 0)
    for d in (1, 7, 2, 6):
        pass_on(0, d)
    for i in range(HANDED_ALONG_Z):
        tile_arrival(0, i).wait_recv()
        hand_copy(i).start()

    loads[7].wait()
    for j in range(1, 4):
        cols_arrival(j).wait_recv()
    to_smem = pltpu.make_async_copy(cols_t, cols_s, loc.at[9])
    to_smem.start()

    for i in range(4):
        loads[i].wait()
    feat2 = feat_v[...].reshape(256, 512)
    cot2 = cot_v[...]
    self_part[...] = dot(feat2, w_self[...])
    cot_part[...] = dot_bt(cot2, w_out[...])

    for d in (1, 7, 2, 6):
        pass_on(1, d)
    for i in range(HANDED_ALONG_Z, 4):
        tile_arrival(1, i).wait_recv()
        hand_copy(i).start()

    to_smem.wait()
    lane = lax.broadcasted_iota(jnp.int32, (8, 128), 1)
    start = jnp.zeros((8, 128), jnp.int32)
    slots = []
    for e in range(64):
        index = window_index(cols_s[e // 16, (e // 8) % 2, e % 8], g)
        slots.append(index)
        start = start + (index < lane).astype(jnp.int32)
        keys[e : e + 1, :] = jnp.full((1, 128), index * 64 + e, jnp.int32)
    all_keys = keys[...]
    rank = jnp.zeros((64, 128), jnp.int32)
    for e in range(64):
        rank = rank + (all_keys > slots[e] * 64 + e).astype(jnp.int32)
    lane64 = lax.broadcasted_iota(jnp.int32, (64, 128), 1)
    entry = lax.broadcasted_iota(jnp.int32, (64, 128), 0)
    order = jnp.sum(jnp.where(rank == lane64, entry, 0), axis=0, keepdims=True)
    table[0:8, :] = jnp.broadcast_to(order, (8, 128))
    table[8:16, :] = start
    to_smem = pltpu.make_async_copy(table, table_s, loc.at[10])
    to_smem.start()
    to_smem.wait()

    for d in (3, 5, 4):
        for row in range(2):
            pass_on(row, d)
    loads[6].wait()
    for i in range(HANDED_ALONG_Z, 4):
        tile_arrival(0, i).wait_recv()
    for i in range(HANDED_ALONG_Z):
        tile_arrival(1, i).wait_recv()
    for i in range(4):
        hand_arrival(i).wait_recv()
    for d in range(8):
        for row in range(2):
            for copy in ring_arrivals(row, d):
                copy.wait_recv()

    def agg_copy(j):
        part, peer = team(j)
        return remote(
            aggq.at[pl.ds(part * 2, 2)], aggr.at[:, :, lanes(f)], sa.at[j], ra.at[j], g, peer
        )

    def agg_arrival(j):
        part, peer = team(4 - j)
        view = aggr.at[:, :, lanes(part)]
        return remote(view, view, sa.at[j], ra.at[j], g, peer)

    def block_sum(part, half_of):
        picked = [win[window_index(cols_s[part, half_of, k], g)] for k in range(8)]
        left = jnp.concatenate([tiles_t[part * 16 + half_of * 8 + k] for k in range(8)], axis=1)
        return dot(left, jnp.concatenate(picked, axis=0)).astype(BF)

    for j in (1, 2, 3, 0):
        part = team(j)[0]
        for half_of in range(2):
            summed = block_sum(part, half_of)
            if j:
                aggq[part * 2 + half_of] = summed
            else:
                aggr[half_of, :, lanes(f)] = summed
        if j:
            agg_copy(j).start()
    loads[4].wait()
    loads[5].wait()
    for j in range(1, 4):
        agg_arrival(j).wait_recv()

    agg = aggr[...].reshape(256, 512)
    pre_first = dot(agg, w_agg[...]) + self_part[...]
    first = (pre_first * jax.nn.sigmoid(pre_first)).astype(BF)
    pre_second = dot(first, w_mid[...])
    second = (pre_second * jax.nn.sigmoid(pre_second)).astype(BF)
    delta_second = (cot_part[...] * silu_slope(pre_second)).astype(BF)
    delta_first = (dot_bt(delta_second, w_mid[...]) * silu_slope(pre_first)).astype(BF)
    dagg[...] = dot_bt(delta_first, w_agg[...]).astype(BF).reshape(2, 128, 512)

    def delta_copy(j):
        part, peer = team(j)
        return remote(
            dagg.at[:, :, lanes(part)], delt.at[pl.ds(f * 2, 2)], sd.at[j], rd.at[j], g, peer
        )

    def delta_arrival(j):
        part, peer = team(4 - j)
        view = delt.at[pl.ds(part * 2, 2)]
        return remote(view, view, sd.at[j], rd.at[j], g, peer)

    for j in range(1, 4):
        delta_copy(j).start()
    delt[pl.ds(f * 2, 2)] = dagg[:, :, lanes(f)]

    def core_copy(m):
        return remote(grads.at[m, :, lanes(1 - core, 256)], half_in.at[m], s_core.at[m], r_core.at[m], sibling, r)

    for m, (a, b) in enumerate(((second, cot2), (first, delta_second), (agg, delta_first), (feat2, delta_first))):
        grads[m] = dot_at(a, b).astype(BF)
        core_copy(m).start()
    upd[...] = (feat2.astype(F32) + dot(second, w_out[...])).astype(BF)
    base[...] = (cot2.astype(F32) + dot_bt(delta_first, w_self[...])).reshape(2, 128, 512)

    for m in range(4):
        core_copy(m).wait_recv()
        half[m] = (grads[m, :, lanes(core, 256)].astype(F32) + half_in[m].astype(F32)).astype(BF)

    def y_copy(j):
        row, rep = across if j & 2 else g, y_mate if j & 1 else r
        rows = pl.ds(pl.multiple_of((rep // 8) * 256, 256), 256)
        return remote(half.at[:, rows, lanes(row // 8)], pair_in.at[j - 1], s_pair.at[j], r_pair.at[j], row, rep)

    for j in range(1, 4):
        y_copy(j).start()

    for j in range(1, 4):
        delta_arrival(j).wait_recv()

    csum[0] = jnp.zeros((128, 128), F32)

    def add_tiles(i, running):
        for step in range(4):
            e = table_s[0, i * 4 + step]
            running = running + dot_at(tiles_t[e], delt[lax.div(e, 8)])
            csum[i * 4 + step + 1] = running
        return running

    lax.fori_loop(0, 16, add_tiles, jnp.zeros((128, 128), F32))

    def message(w):
        return csum[table_s[8, w + 1]] - csum[table_s[8, w]]

    def message_copies(o):
        s = wrap16(r + o)
        rows = pl.ds(s * 2, 2)
        return (
            remote(to_prior.at[rows], from_next.at[rows], sm.at[0, o], rm.at[0, o], down, r),
            remote(to_next.at[rows], from_prior.at[rows], sm.at[1, o], rm.at[1, o], up, r),
        )

    def message_arrivals(o):
        s = wrap16(r + o)
        a = from_next.at[pl.ds(s * 2, 2)]
        b = from_prior.at[pl.ds(s * 2, 2)]
        return (
            remote(a, a, sm.at[0, o], rm.at[0, o], up, r),
            remote(b, b, sm.at[1, o], rm.at[1, o], down, r),
        )

    @pl.loop(0, 16)
    def _(i):
        o = lax.rem(i + 1, 16)
        s = wrap16(r + o)
        for part in range(2):
            to_prior[s * 2 + part] = message(s * 2 + part).astype(BF)
            to_next[s * 2 + part] = message(64 + s * 2 + part).astype(BF)
        for copy in message_copies(o):
            copy.start()

    def return_copy(o):
        s = wrap16(r + o)
        return remote(sums.at[pl.ds(s * 2, 2)], parts.at[pl.ds(r * 2, 2)], sp.at[o], rp.at[o], g, s)

    def return_arrival(o):
        s = wrap16(r - o)
        view = parts.at[pl.ds(s * 2, 2)]
        return remote(view, view, sp.at[o], rp.at[o], g, s)

    def total(s, part):
        i = s * 2 + part
        return (message(32 + i) + from_next[i].astype(F32) + from_prior[i].astype(F32)).astype(BF)

    def send_back(o):
        for copy in message_arrivals(o):
            copy.wait_recv()
        s = wrap16(r + o)
        for part in range(2):
            sums[s * 2 + part] = total(s, part)
        return_copy(o).start()

    pl.loop(1, Y_SUM_AT)(send_back)
    for j in range(1, 4):
        y_copy(j).wait_recv()
    own_rows = pl.ds(pl.multiple_of(y * 256, 256), 256)
    for m in range(4):
        value = half[m, own_rows, lanes(y_hi)].astype(F32)
        for j in range(3):
            value = value + pair_in[j, m].astype(F32)
        pair[m] = value.astype(BF)

    def x_row(j):
        return y_hi * 8 + ((x + j) % 4) * 2 + core

    def x_copy(j):
        return remote(pair.at[(x + j) % 4], ring_in.at[j - 1], s_ring.at[j], r_ring.at[j], x_row(j), r)

    for j in range(1, 4):
        x_copy(j).start()
    pl.loop(Y_SUM_AT, X_SUM_AT)(send_back)
    for j in range(1, 4):
        x_copy(j).wait_recv()
    ring[...] = (
        pair[x].astype(F32) + ring_in[0].astype(F32) + ring_in[1].astype(F32) + ring_in[2].astype(F32)
    ).astype(BF)

    def rep_copy(d):
        to = (z + d) % 8
        rows = pl.ds(pl.multiple_of(to * 32, 32), 32)
        return remote(ring.at[rows], rep_in.at[d], s_rep.at[d], r_rep.at[d], g, y * 8 + to)

    for d in range(1, 8):
        rep_copy(d).start()
    pl.loop(X_SUM_AT, 16)(send_back)
    for copy in message_arrivals(0):
        copy.wait_recv()
    for part in range(2):
        parts[r * 2 + part] = total(r, part)

    acc = ring[pl.ds(pl.multiple_of(z * 32, 32), 32)].astype(F32)
    for d in range(1, 8):
        rep_copy(d).wait_recv()
        acc = acc + rep_in[d].astype(F32)
    piece[...] = acc * scale

    def place(row):
        return gout.at[(row // 2) % 4, :, lanes((row % 2) * 2 + row // 8)]

    def row_copy(o):
        return remote(piece, place(g), s_row.at[o], r_row.at[o], wrap16(g + o), r)

    def row_arrival(o):
        src = wrap16(g - o)
        return remote(piece, place(src), s_row.at[o], r_row.at[o], src, r)

    @pl.loop(1, 16)
    def _(o):
        row_copy(o).start()

    gout[x, :, lanes(core * 2 + y_hi)] = piece[...]

    @pl.loop(1, 16)
    def _(o):
        return_arrival(o).wait_recv()

    for q in range(4):
        cut = slice(q * 128, q * 128 + 128)
        value = base[:, :, cut]
        for t in range(4):
            s = (q // 2) * 8 + 2 * t + q % 2
            value = value + parts[2 * s : 2 * s + 2].astype(F32)
        gf[:, :, cut] = value.astype(BF)

    @pl.loop(1, 16)
    def _(o):
        row_arrival(o).wait_recv()

    @pl.loop(0, 16)
    def _(o):
        for copy in message_copies(o):
            copy.wait_send()

    @pl.loop(1, 16)
    def _(o):
        return_copy(o).wait_send()
        row_copy(o).wait_send()

    mate_copy().wait_send()
    for row in range(2):
        for d in (1, 7, 2, 6):
            chunk_copy(row, d).wait_send()
        chunk_copy(row, 3, held=1).wait_send()
        chunk_copy(row, 5, held=7).wait_send()
        chunk_copy(row, 4, held=2 if row == 0 else 6).wait_send()
        for d in range(8):
            for copy in ring_copies(row, d):
                copy.wait_send()
    for i in range(4):
        tile_copy(0, i).wait_send()
        tile_copy(1, i).wait_send()
        hand_copy(i).wait_send()
    for m in range(4):
        core_copy(m).wait_send()
    for j in range(1, 4):
        y_copy(j).wait_send()
        x_copy(j).wait_send()
        cols_copy(j).wait_send()
        agg_copy(j).wait_send()
        delta_copy(j).wait_send()
    for d in range(1, 8):
        rep_copy(d).wait_send()


def shape(dims, kind):
    return jax.ShapeDtypeStruct(dims, kind)


def local(features, tiles, columns, w_aggregate, w_self, w_middle, w_output, cotangent):
    scale = 1.0 / math.sqrt(features.shape[0] * lax.axis_size("row") * lax.axis_size("rep"))
    weight = VMEM((512, 512), BF)
    panel = VMEM((32, 128, 128), BF)
    upd, gf, gout = pl.pallas_call(
        lambda *refs: layer_kernel(scale, *refs),
        out_shape=(shape((256, 512), BF), shape((2, 128, 512), BF), shape((4, 32, 512), F32)),
        in_specs=[pl.BlockSpec(memory_space=pltpu.HBM)] * 8,
        out_specs=[pl.BlockSpec(memory_space=VMEM)] * 3,
        scratch_shapes=[
            VMEM((2, 128, 512), BF), VMEM((256, 512), BF), weight, weight, weight, weight,
            VMEM((64, 128, 128), BF), VMEM((4, 2, 8), jnp.int32), VMEM((96, 128, 128), BF),
            pltpu.SMEM((4, 2, 8), jnp.int32), VMEM((64, 128), jnp.int32),
            VMEM((16, 128), jnp.int32), pltpu.SMEM((16, 128), jnp.int32),
            VMEM((8, 128, 128), BF), VMEM((2, 128, 512), BF), VMEM((2, 128, 512), BF),
            VMEM((8, 128, 128), BF), VMEM((256, 512), F32), VMEM((256, 512), F32),
            VMEM((2, 128, 512), F32), VMEM((4, 512, 512), BF), VMEM((65, 128, 128), F32),
            panel, panel, panel, panel, panel, panel,
            VMEM((4, 512, 256), BF), VMEM((4, 512, 256), BF), VMEM((3, 256, 128), BF), VMEM((256, 128), BF),
            VMEM((3, 4, 256, 128), BF), VMEM((4, 256, 128), BF), VMEM((8, 32, 128), BF), VMEM((32, 128), F32),
            VMEM((2, 128, 256), BF),
            DMA((12,)), DMA, DMA,
            DMA((2, 8)), DMA((2, 8)),
            DMA((2, 8, 2)), DMA((2, 8, 2)),
            DMA((3, 4)), DMA((3, 4)),
            DMA((4,)), DMA((4,)),
            DMA((4,)), DMA((4,)),
            DMA((4,)), DMA((4,)),
            DMA((2, 16)), DMA((2, 16)),
            DMA((16,)), DMA((16,)),
            DMA((4,)), DMA((4,)),
            DMA((4,)), DMA((4,)),
            DMA((4,)), DMA((4,)),
            DMA((8,)), DMA((8,)),
            DMA((16,)), DMA((16,)),
        ],
        compiler_params=pltpu.CompilerParams(
            collective_id=0, has_side_effects=True, vmem_limit_bytes=52 * 1024 * 1024
        ),
        name="message_passing_layer",
    )(
        *(
            pltpu.with_memory_space_constraint(value, pltpu.HBM)
            for value in (
                features.reshape(2, 128, 512), tiles.reshape(16, 128, 128), columns,
                w_aggregate, w_self, w_middle, w_output, cotangent,
            )
        )
    )
    return upd, gf.reshape(256, 512), gout[0], gout[1], gout[2], gout[3]


def solution(mesh):
    placed = (
        P(("row", "rep"), None),
        P(("row", "rep"), None, None, None),
        P(("row", "rep"), None),
        P(),
        P(),
        P(),
        P(),
        P(("row", "rep"), None),
    )
    return jax.shard_map(
        local,
        mesh=mesh,
        in_specs=placed,
        out_specs=(
            P(("row", "rep"), None),
            P(("row", "rep"), None),
            P("rep", None),
            P("rep", None),
            P("rep", None),
            P("rep", None),
        ),
        check_vma=False,
    )
```

```python
import math

import jax
import jax.numpy as jnp
from jax import lax
from jax.experimental import pallas as pl
from jax.experimental.pallas import tpu as pltpu
from jax.sharding import PartitionSpec as P

MESH = pl.DeviceIdType.MESH
BF = jnp.bfloat16
F32 = jnp.float32
VMEM = pltpu.VMEM
DMA = pltpu.SemaphoreType.DMA
HANDED_ALONG_Z = 2
Y_SUM_AT, X_SUM_AT = 8, 12


def wrap16(value):
    return lax.rem(value + 16, 16)


def quarter(rep):
    return (rep // 8) * 2 + rep % 2


def mate(rep, core, part):
    z = rep % 8
    step = jnp.where((z + core) % 2 == 0, 1, 7)
    other = (z + step) % 8
    return (part // 2) * 8 + jnp.where(z % 2 == part % 2, z, other)


def lanes(part, size=128):
    return pl.ds(pl.multiple_of(part * size, size), size)


def remote(src, dst, send, recv, row, rep):
    return pltpu.make_async_remote_copy(
        src_ref=src, dst_ref=dst, send_sem=send, recv_sem=recv, device_id=(row, rep), device_id_type=MESH
    )


def window_index(column, group):
    panel = jnp.minimum(lax.rem(lax.div(column, 32) - group + 17, 16), 2)
    return panel * 32 + lax.rem(column, 32)


def dot(a, b):
    return jnp.dot(a, b, preferred_element_type=F32)


def dot_bt(a, b):
    return lax.dot_general(a, b, (((1,), (1,)), ((), ())), preferred_element_type=F32)


def dot_at(a, b):
    return lax.dot_general(a, b, (((0,), (0,)), ((), ())), preferred_element_type=F32)


def silu_slope(value):
    sig = jax.nn.sigmoid(value)
    return sig * (1.0 + value * (1.0 - sig))


def greet(peers):
    barrier = pltpu.get_barrier_semaphore()
    for row, rep in peers:
        pl.semaphore_signal(barrier, inc=1, device_id=(row, rep), device_id_type=MESH)
    pl.semaphore_wait(barrier, len(peers))


def layer_kernel(
    scale,
    feat, tiles, cols, w_agg_h, w_self_h, w_mid_h, w_out_h, cot_h,
    upd, gf, gout,
    feat_v, cot_v, w_agg, w_self, w_mid, w_out,
    tiles_t, cols_t, win, cols_s, keys, table, table_s, aggq, aggr, dagg, delt, self_part, cot_part,
    base, grads, csum, to_next, to_prior, from_prior, from_next, sums, parts,
    half_in, half, a_in, b_in, a_sum, b_sum, a2_in, b2_in, last, rep_in, piece,
    from_mate, loc, s_mate, r_mate, s1, r1, sx, rx, st, rt, sc, rc, sa, ra, sd, rd,
    sm, rm, sp, rp, s_core, r_core, s_a, r_a, s_b, r_b, s_a2, r_a2, s_b2, r_b2, s_rep, r_rep, s_row, r_row,
):
    g = lax.axis_index("row")
    r = lax.axis_index("rep")
    core = g % 2
    x = (g // 2) % 4
    y_hi = g // 8
    f = quarter(r)
    up, down = wrap16(g + 1), wrap16(g - 1)
    sibling = g + 1 - 2 * core
    across = (g + 8) % 16
    y, z = r // 8, r % 8
    y_mate = (1 - y) * 8 + z
    z_mate = y * 8 + (z + jnp.where((z + core) % 2 == 0, 1, 7)) % 8

    loads = [
        pltpu.make_async_copy(src, dst, loc.at[i])
        for i, (src, dst) in enumerate(
            (
                (feat, feat_v), (w_self_h, w_self), (cot_h, cot_v), (w_out_h, w_out),
                (w_agg_h, w_agg), (w_mid_h, w_mid),
                (tiles, tiles_t.at[pl.ds(f * 16, 16)]), (cols, cols_t.at[f]),
            )
        )
    ]
    for load in loads:
        load.start()
    greet([(g, wrap16(r + o)) for o in range(1, 16)] + [(wrap16(g + o), r) for o in range(1, 16)] + [(across, y_mate)])

    def slot(panel, rep):
        return win.at[pl.ds(panel * 32 + rep * 2, 2)]

    def source(row, d):
        return jnp.where(row == 0, y, 1 - y) * 8 + (z - d + 8) % 8

    def mate_copy():
        return remote(feat.at[:, :, lanes(1 - y, 256)], from_mate, s_mate, r_mate, g, y_mate)

    def chunk_copy(row, d, held=0):
        peer = y * 8 + (z - held + d) % 8
        if held:
            src = slot(1, source(row, held))
        else:
            src = (feat, from_mate)[row].at[:, :, lanes(quarter(peer) if row == 0 else peer % 2)]
        dst = slot(1, source(row, held))
        return remote(src, dst, s1.at[row, d], r1.at[row, d], g, peer)

    def chunk_arrival(row, d):
        view = slot(1, source(row, d))
        return remote(view, view, s1.at[row, d], r1.at[row, d], g, y * 8 + (z - d + 8) % 8)

    def ring_copies(row, d):
        src = source(row, d)
        return (
            remote(slot(1, src), slot(0, src), sx.at[row, d, 0], rx.at[row, d, 0], up, r),
            remote(slot(1, src), slot(2, src), sx.at[row, d, 1], rx.at[row, d, 1], down, r),
        )

    def ring_arrivals(row, d):
        src = source(row, d)
        return (
            remote(slot(0, src), slot(0, src), sx.at[row, d, 0], rx.at[row, d, 0], down, r),
            remote(slot(2, src), slot(2, src), sx.at[row, d, 1], rx.at[row, d, 1], up, r),
        )

    def send_ring(row, d):
        for copy in ring_copies(row, d):
            copy.start()

    def pass_on(row, d):
        chunk_arrival(row, d).wait_recv()
        if d in (1, 7):
            chunk_copy(row, 3 if d == 1 else 5, held=d).start()
        if d == (2 if row == 0 else 6):
            chunk_copy(row, 4, held=d).start()
        send_ring(row, d)

    def team(j):
        part = (f + j) % 4
        return part, mate(r, core, part)

    def cols_copy(j):
        return remote(cols, cols_t.at[f], sc.at[j], rc.at[j], g, team(j)[1])

    def cols_arrival(j):
        part, peer = team(4 - j)
        return remote(cols_t.at[part], cols_t.at[part], sc.at[j], rc.at[j], g, peer)

    def piece_of(rep, i):
        return tiles_t.at[pl.ds(quarter(rep) * 16 + i * 4, 4)]

    def tile_copy(way, i):
        peer = (y_mate, z_mate)[way]
        return remote(tiles.at[pl.ds(i * 4, 4)], piece_of(r, i), st.at[way, i], rt.at[way, i], g, peer)

    def tile_arrival(way, i):
        peer = (y_mate, z_mate)[way]
        return remote(piece_of(peer, i), piece_of(peer, i), st.at[way, i], rt.at[way, i], g, peer)

    def hand_copy(i):
        src, peer = (y_mate, z_mate) if i < HANDED_ALONG_Z else (z_mate, y_mate)
        return remote(piece_of(src, i), piece_of(src, i), st.at[2, i], rt.at[2, i], g, peer)

    def hand_arrival(i):
        far = mate(r, core, 3 - f)
        peer = z_mate if i < HANDED_ALONG_Z else y_mate
        return remote(piece_of(far, i), piece_of(far, i), st.at[2, i], rt.at[2, i], g, peer)

    for j in range(1, 4):
        cols_copy(j).start()

    mate_copy().start()
    for d in (1, 7, 2, 6):
        chunk_copy(0, d).start()
    for i in range(4):
        tile_copy(0, i).start()
    for i in range(HANDED_ALONG_Z, 4):
        tile_copy(1, i).start()
    own = pltpu.make_async_copy(feat.at[:, :, lanes(f)], slot(1, r), loc.at[8])
    own.start()
    own.wait()
    send_ring(0, 0)
    mate_copy().wait_recv()
    for d in (1, 7, 2, 6):
        chunk_copy(1, d).start()
    for i in range(HANDED_ALONG_Z):
        tile_copy(1, i).start()
    own = pltpu.make_async_copy(from_mate.at[:, :, lanes(z % 2)], slot(1, y_mate), loc.at[11])
    own.start()
    own.wait()
    send_ring(1, 0)
    for d in (1, 7, 2, 6):
        pass_on(0, d)
    for i in range(HANDED_ALONG_Z):
        tile_arrival(0, i).wait_recv()
        hand_copy(i).start()

    loads[7].wait()
    for j in range(1, 4):
        cols_arrival(j).wait_recv()
    to_smem = pltpu.make_async_copy(cols_t, cols_s, loc.at[9])
    to_smem.start()

    for i in range(4):
        loads[i].wait()
    feat2 = feat_v[...].reshape(256, 512)
    cot2 = cot_v[...]
    self_part[...] = dot(feat2, w_self[...])
    cot_part[...] = dot_bt(cot2, w_out[...])

    for d in (1, 7, 2, 6):
        pass_on(1, d)
    for i in range(HANDED_ALONG_Z, 4):
        tile_arrival(1, i).wait_recv()
        hand_copy(i).start()

    to_smem.wait()
    lane = lax.broadcasted_iota(jnp.int32, (8, 128), 1)
    start = jnp.zeros((8, 128), jnp.int32)
    slots = []
    for e in range(64):
        index = window_index(cols_s[e // 16, (e // 8) % 2, e % 8], g)
        slots.append(index)
        start = start + (index < lane).astype(jnp.int32)
        keys[e : e + 1, :] = jnp.full((1, 128), index * 64 + e, jnp.int32)
    all_keys = keys[...]
    rank = jnp.zeros((64, 128), jnp.int32)
    for e in range(64):
        rank = rank + (all_keys > slots[e] * 64 + e).astype(jnp.int32)
    lane64 = lax.broadcasted_iota(jnp.int32, (64, 128), 1)
    entry = lax.broadcasted_iota(jnp.int32, (64, 128), 0)
    order = jnp.sum(jnp.where(rank == lane64, entry, 0), axis=0, keepdims=True)
    table[0:8, :] = jnp.broadcast_to(order, (8, 128))
    table[8:16, :] = start
    to_smem = pltpu.make_async_copy(table, table_s, loc.at[10])
    to_smem.start()
    to_smem.wait()

    for d in (3, 5, 4):
        for row in range(2):
            pass_on(row, d)
    loads[6].wait()
    for i in range(HANDED_ALONG_Z, 4):
        tile_arrival(0, i).wait_recv()
    for i in range(HANDED_ALONG_Z):
        tile_arrival(1, i).wait_recv()
    for i in range(4):
        hand_arrival(i).wait_recv()
    for d in range(8):
        for row in range(2):
            for copy in ring_arrivals(row, d):
                copy.wait_recv()

    def agg_copy(j):
        part, peer = team(j)
        return remote(
            aggq.at[pl.ds(part * 2, 2)], aggr.at[:, :, lanes(f)], sa.at[j], ra.at[j], g, peer
        )

    def agg_arrival(j):
        part, peer = team(4 - j)
        view = aggr.at[:, :, lanes(part)]
        return remote(view, view, sa.at[j], ra.at[j], g, peer)

    def block_sum(part, half_of):
        picked = [win[window_index(cols_s[part, half_of, k], g)] for k in range(8)]
        left = jnp.concatenate([tiles_t[part * 16 + half_of * 8 + k] for k in range(8)], axis=1)
        return dot(left, jnp.concatenate(picked, axis=0)).astype(BF)

    for j in (1, 2, 3, 0):
        part = team(j)[0]
        for half_of in range(2):
            summed = block_sum(part, half_of)
            if j:
                aggq[part * 2 + half_of] = summed
            else:
                aggr[half_of, :, lanes(f)] = summed
        if j:
            agg_copy(j).start()
    loads[4].wait()
    loads[5].wait()
    for j in range(1, 4):
        agg_arrival(j).wait_recv()

    agg = aggr[...].reshape(256, 512)
    pre_first = dot(agg, w_agg[...]) + self_part[...]
    first = (pre_first * jax.nn.sigmoid(pre_first)).astype(BF)
    pre_second = dot(first, w_mid[...])
    second = (pre_second * jax.nn.sigmoid(pre_second)).astype(BF)
    delta_second = (cot_part[...] * silu_slope(pre_second)).astype(BF)
    delta_first = (dot_bt(delta_second, w_mid[...]) * silu_slope(pre_first)).astype(BF)
    dagg[...] = dot_bt(delta_first, w_agg[...]).astype(BF).reshape(2, 128, 512)

    def delta_copy(j):
        part, peer = team(j)
        return remote(
            dagg.at[:, :, lanes(part)], delt.at[pl.ds(f * 2, 2)], sd.at[j], rd.at[j], g, peer
        )

    def delta_arrival(j):
        part, peer = team(4 - j)
        view = delt.at[pl.ds(part * 2, 2)]
        return remote(view, view, sd.at[j], rd.at[j], g, peer)

    for j in range(1, 4):
        delta_copy(j).start()
    delt[pl.ds(f * 2, 2)] = dagg[:, :, lanes(f)]

    def core_copy(m):
        return remote(grads.at[m, :, lanes(1 - core, 256)], half_in.at[m], s_core.at[m], r_core.at[m], sibling, r)

    for m, (a, b) in enumerate(((second, cot2), (first, delta_second), (agg, delta_first), (feat2, delta_first))):
        grads[m] = dot_at(a, b).astype(BF)
        core_copy(m).start()
    upd[...] = (feat2.astype(F32) + dot(second, w_out[...])).astype(BF)
    base[...] = (cot2.astype(F32) + dot_bt(delta_first, w_self[...])).reshape(2, 128, 512)

    for m in range(4):
        core_copy(m).wait_recv()
        value = (grads[m, :, lanes(core, 256)].astype(F32) + half_in[m].astype(F32)).astype(BF)
        half[m] = value.reshape(16, 2, 16, 256)

    def y_peer(j):
        return across if j & 2 else g, y_mate if j & 1 else r

    def y_part(row, rep):
        return pl.ds((rep // 8) * 8, 8), lanes(row // 8)

    def x_peer(j):
        to = (x + j) % 4
        return y_hi * 8 + to * 2 + core, to

    def a_copy(j):
        row, rep = y_peer(j)
        rows, columns = y_part(row, rep)
        src = half.at[0:2, rows, :, :, columns]
        return remote(src, a_in.at[j - 1], s_a.at[j], r_a.at[j], row, rep)

    def b_copy(j):
        row, to = x_peer(j)
        src = half.at[2 + to // 2, :, to % 2]
        return remote(src, b_in.at[j - 1], s_b.at[j], r_b.at[j], row, r)

    def a2_copy(j):
        row, to = x_peer(j)
        return remote(a_sum.at[to // 2, :, to % 2], a2_in.at[j - 1], s_a2.at[j], r_a2.at[j], row, r)

    def b2_copy(j):
        row, rep = y_peer(j)
        rows, columns = y_part(row, rep)
        return remote(b_sum.at[rows, :, columns], b2_in.at[j - 1], s_b2.at[j], r_b2.at[j], row, rep)

    own_rows, own_columns = y_part(g, r)
    for j in range(1, 4):
        a_copy(j).start()
        b_copy(j).start()

    for j in range(1, 4):
        delta_arrival(j).wait_recv()

    csum[0] = jnp.zeros((128, 128), F32)

    def add_tiles(i, running):
        for step in range(4):
            e = table_s[0, i * 4 + step]
            running = running + dot_at(tiles_t[e], delt[lax.div(e, 8)])
            csum[i * 4 + step + 1] = running
        return running

    lax.fori_loop(0, 16, add_tiles, jnp.zeros((128, 128), F32))

    def message(w):
        return csum[table_s[8, w + 1]] - csum[table_s[8, w]]

    def message_copies(o):
        s = wrap16(r + o)
        rows = pl.ds(s * 2, 2)
        return (
            remote(to_prior.at[rows], from_next.at[rows], sm.at[0, o], rm.at[0, o], down, r),
            remote(to_next.at[rows], from_prior.at[rows], sm.at[1, o], rm.at[1, o], up, r),
        )

    def message_arrivals(o):
        s = wrap16(r + o)
        a = from_next.at[pl.ds(s * 2, 2)]
        b = from_prior.at[pl.ds(s * 2, 2)]
        return (
            remote(a, a, sm.at[0, o], rm.at[0, o], up, r),
            remote(b, b, sm.at[1, o], rm.at[1, o], down, r),
        )

    @pl.loop(0, 16)
    def _(i):
        o = lax.rem(i + 1, 16)
        s = wrap16(r + o)
        for part in range(2):
            to_prior[s * 2 + part] = message(s * 2 + part).astype(BF)
            to_next[s * 2 + part] = message(64 + s * 2 + part).astype(BF)
        for copy in message_copies(o):
            copy.start()

    def return_copy(o):
        s = wrap16(r + o)
        return remote(sums.at[pl.ds(s * 2, 2)], parts.at[pl.ds(r * 2, 2)], sp.at[o], rp.at[o], g, s)

    def return_arrival(o):
        s = wrap16(r - o)
        view = parts.at[pl.ds(s * 2, 2)]
        return remote(view, view, sp.at[o], rp.at[o], g, s)

    def total(s, part):
        i = s * 2 + part
        return (message(32 + i) + from_next[i].astype(F32) + from_prior[i].astype(F32)).astype(BF)

    def send_back(o):
        for copy in message_arrivals(o):
            copy.wait_recv()
        s = wrap16(r + o)
        for part in range(2):
            sums[s * 2 + part] = total(s, part)
        return_copy(o).start()

    pl.loop(1, Y_SUM_AT)(send_back)
    for j in range(1, 4):
        a_copy(j).wait_recv()
        b_copy(j).wait_recv()
    for m in range(2):
        value = half[m, own_rows, :, :, own_columns].astype(F32)
        for j in range(3):
            value = value + a_in[j, m].astype(F32)
        a_sum[m] = value.astype(BF)
    value = half[2 + x // 2, :, x % 2].astype(F32)
    for j in range(3):
        value = value + b_in[j].astype(F32)
    b_sum[...] = value.astype(BF)
    for j in range(1, 4):
        a2_copy(j).start()
        b2_copy(j).start()
    pl.loop(Y_SUM_AT, X_SUM_AT)(send_back)
    for j in range(1, 4):
        a2_copy(j).wait_recv()
        b2_copy(j).wait_recv()
    a_value = a_sum[x // 2, :, x % 2].astype(F32)
    b_value = b_sum[own_rows, :, own_columns].astype(F32)
    for j in range(3):
        a_value = a_value + a2_in[j].astype(F32)
        b_value = b_value + b2_in[j].astype(F32)
    last[:, 0] = a_value.astype(BF)
    last[:, 1] = b_value.astype(BF)

    def rep_copy(d):
        to = (z + d) % 8
        return remote(last.at[to], rep_in.at[d], s_rep.at[d], r_rep.at[d], g, y * 8 + to)

    for d in range(1, 8):
        rep_copy(d).start()
    pl.loop(X_SUM_AT, 16)(send_back)
    for copy in message_arrivals(0):
        copy.wait_recv()
    for part in range(2):
        parts[r * 2 + part] = total(r, part)

    acc = last[z].astype(F32)
    for d in range(1, 8):
        rep_copy(d).wait_recv()
        acc = acc + rep_in[d].astype(F32)
    piece[...] = acc * scale

    def place(row):
        to = (row // 2) % 4
        rows = pl.ds(pl.multiple_of((to % 2) * 16, 16), 16)
        return gout.at[:, to // 2, rows, lanes((row % 2) * 2 + row // 8)]

    def row_copy(o):
        return remote(piece, place(g), s_row.at[o], r_row.at[o], wrap16(g + o), r)

    def row_arrival(o):
        src = wrap16(g - o)
        return remote(piece, place(src), s_row.at[o], r_row.at[o], src, r)

    @pl.loop(1, 16)
    def _(o):
        row_copy(o).start()

    rows = pl.ds(pl.multiple_of((x % 2) * 16, 16), 16)
    gout[:, x // 2, rows, lanes(core * 2 + y_hi)] = piece[...]

    @pl.loop(1, 16)
    def _(o):
        return_arrival(o).wait_recv()

    for q in range(4):
        cut = slice(q * 128, q * 128 + 128)
        value = base[:, :, cut]
        for t in range(4):
            s = (q // 2) * 8 + 2 * t + q % 2
            value = value + parts[2 * s : 2 * s + 2].astype(F32)
        gf[:, :, cut] = value.astype(BF)

    @pl.loop(1, 16)
    def _(o):
        row_arrival(o).wait_recv()

    @pl.loop(0, 16)
    def _(o):
        for copy in message_copies(o):
            copy.wait_send()

    @pl.loop(1, 16)
    def _(o):
        return_copy(o).wait_send()
        row_copy(o).wait_send()

    mate_copy().wait_send()
    for row in range(2):
        for d in (1, 7, 2, 6):
            chunk_copy(row, d).wait_send()
        chunk_copy(row, 3, held=1).wait_send()
        chunk_copy(row, 5, held=7).wait_send()
        chunk_copy(row, 4, held=2 if row == 0 else 6).wait_send()
        for d in range(8):
            for copy in ring_copies(row, d):
                copy.wait_send()
    for i in range(4):
        tile_copy(0, i).wait_send()
        tile_copy(1, i).wait_send()
        hand_copy(i).wait_send()
    for m in range(4):
        core_copy(m).wait_send()
    for j in range(1, 4):
        a_copy(j).wait_send()
        b_copy(j).wait_send()
        a2_copy(j).wait_send()
        b2_copy(j).wait_send()
        cols_copy(j).wait_send()
        agg_copy(j).wait_send()
        delta_copy(j).wait_send()
    for d in range(1, 8):
        rep_copy(d).wait_send()


def shape(dims, kind):
    return jax.ShapeDtypeStruct(dims, kind)


def local(features, tiles, columns, w_aggregate, w_self, w_middle, w_output, cotangent):
    scale = 1.0 / math.sqrt(features.shape[0] * lax.axis_size("row") * lax.axis_size("rep"))
    weight = VMEM((512, 512), BF)
    panel = VMEM((32, 128, 128), BF)
    upd, gf, gout = pl.pallas_call(
        lambda *refs: layer_kernel(scale, *refs),
        out_shape=(shape((256, 512), BF), shape((2, 128, 512), BF), shape((2, 2, 32, 512), F32)),
        in_specs=[pl.BlockSpec(memory_space=pltpu.HBM)] * 8,
        out_specs=[pl.BlockSpec(memory_space=VMEM)] * 3,
        scratch_shapes=[
            VMEM((2, 128, 512), BF), VMEM((256, 512), BF), weight, weight, weight, weight,
            VMEM((64, 128, 128), BF), VMEM((4, 2, 8), jnp.int32), VMEM((96, 128, 128), BF),
            pltpu.SMEM((4, 2, 8), jnp.int32), VMEM((64, 128), jnp.int32),
            VMEM((16, 128), jnp.int32), pltpu.SMEM((16, 128), jnp.int32),
            VMEM((8, 128, 128), BF), VMEM((2, 128, 512), BF), VMEM((2, 128, 512), BF),
            VMEM((8, 128, 128), BF), VMEM((256, 512), F32), VMEM((256, 512), F32),
            VMEM((2, 128, 512), F32), VMEM((4, 512, 512), BF), VMEM((65, 128, 128), F32),
            panel, panel, panel, panel, panel, panel,
            VMEM((4, 512, 256), BF), VMEM((4, 16, 2, 16, 256), BF),
            VMEM((3, 2, 8, 2, 16, 128), BF), VMEM((3, 16, 16, 256), BF),
            VMEM((2, 8, 2, 16, 128), BF), VMEM((16, 16, 256), BF),
            VMEM((3, 8, 16, 128), BF), VMEM((3, 8, 16, 128), BF),
            VMEM((8, 2, 16, 128), BF), VMEM((8, 2, 16, 128), BF), VMEM((2, 16, 128), F32),
            VMEM((2, 128, 256), BF),
            DMA((12,)), DMA, DMA,
            DMA((2, 8)), DMA((2, 8)),
            DMA((2, 8, 2)), DMA((2, 8, 2)),
            DMA((3, 4)), DMA((3, 4)),
            DMA((4,)), DMA((4,)),
            DMA((4,)), DMA((4,)),
            DMA((4,)), DMA((4,)),
            DMA((2, 16)), DMA((2, 16)),
            DMA((16,)), DMA((16,)),
            DMA((4,)), DMA((4,)),
            DMA((4,)), DMA((4,)),
            DMA((4,)), DMA((4,)),
            DMA((4,)), DMA((4,)),
            DMA((4,)), DMA((4,)),
            DMA((8,)), DMA((8,)),
            DMA((16,)), DMA((16,)),
        ],
        compiler_params=pltpu.CompilerParams(
            collective_id=0, has_side_effects=True, vmem_limit_bytes=52 * 1024 * 1024
        ),
        name="message_passing_layer",
    )(
        *(
            pltpu.with_memory_space_constraint(value, pltpu.HBM)
            for value in (
                features.reshape(2, 128, 512), tiles.reshape(16, 128, 128), columns,
                w_aggregate, w_self, w_middle, w_output, cotangent,
            )
        )
    )
    return upd, gf.reshape(256, 512), gout[0, 0], gout[0, 1], gout[1, 0], gout[1, 1]


def solution(mesh):
    placed = (
        P(("row", "rep"), None),
        P(("row", "rep"), None, None, None),
        P(("row", "rep"), None),
        P(),
        P(),
        P(),
        P(),
        P(("row", "rep"), None),
    )
    return jax.shard_map(
        local,
        mesh=mesh,
        in_specs=placed,
        out_specs=(
            P(("row", "rep"), None),
            P(("row", "rep"), None),
            P("rep", None),
            P("rep", None),
            P("rep", None),
            P("rep", None),
        ),
        check_vma=False,
    )
```

```python
import math

import jax
import jax.numpy as jnp
from jax import lax
from jax.experimental import pallas as pl
from jax.experimental.pallas import tpu as pltpu
from jax.sharding import PartitionSpec as P

MESH = pl.DeviceIdType.MESH
BF = jnp.bfloat16
F32 = jnp.float32
VMEM = pltpu.VMEM
DMA = pltpu.SemaphoreType.DMA
HANDED_ALONG_Z = 2
Y_SUM_AT, X_SUM_AT = 11, 14


def wrap16(value):
    return lax.rem(value + 16, 16)


def quarter(rep):
    return (rep // 8) * 2 + rep % 2


def mate(rep, core, part):
    z = rep % 8
    step = jnp.where((z + core) % 2 == 0, 1, 7)
    other = (z + step) % 8
    return (part // 2) * 8 + jnp.where(z % 2 == part % 2, z, other)


def lanes(part, size=128):
    return pl.ds(pl.multiple_of(part * size, size), size)


def remote(src, dst, send, recv, row, rep):
    return pltpu.make_async_remote_copy(
        src_ref=src, dst_ref=dst, send_sem=send, recv_sem=recv, device_id=(row, rep), device_id_type=MESH
    )


def window_index(column, group):
    panel = jnp.minimum(lax.rem(lax.div(column, 32) - group + 17, 16), 2)
    return panel * 32 + lax.rem(column, 32)


def dot(a, b):
    return jnp.dot(a, b, preferred_element_type=F32)


def dot_bt(a, b):
    return lax.dot_general(a, b, (((1,), (1,)), ((), ())), preferred_element_type=F32)


def dot_at(a, b):
    return lax.dot_general(a, b, (((0,), (0,)), ((), ())), preferred_element_type=F32)


def silu_slope(value):
    sig = jax.nn.sigmoid(value)
    return sig * (1.0 + value * (1.0 - sig))


def greet(peers):
    barrier = pltpu.get_barrier_semaphore()
    for row, rep in peers:
        pl.semaphore_signal(barrier, inc=1, device_id=(row, rep), device_id_type=MESH)
    pl.semaphore_wait(barrier, len(peers))


def layer_kernel(
    scale,
    feat, tiles, cols, w_agg_h, w_self_h, w_mid_h, w_out_h, cot_h,
    upd, gf, gout,
    feat_v, cot_v, w_agg, w_self, w_mid, w_out,
    tiles_t, cols_t, win, cols_s, keys, table, table_s, aggq, aggr, dagg, delt, self_part, cot_part,
    base, grads, csum, to_next, to_prior, from_prior, from_next, sums, parts,
    half_in, half, a_in, b_in, a_sum, b_sum, a2_in, b2_in, last, rep_in, piece,
    from_mate, loc, s_mate, r_mate, s1, r1, sx, rx, st, rt, sc, rc, sa, ra, sd, rd,
    sm, rm, sp, rp, s_core, r_core, s_a, r_a, s_b, r_b, s_a2, r_a2, s_b2, r_b2, s_rep, r_rep, s_row, r_row,
):
    g = lax.axis_index("row")
    r = lax.axis_index("rep")
    core = g % 2
    x = (g // 2) % 4
    y_hi = g // 8
    f = quarter(r)
    up, down = wrap16(g + 1), wrap16(g - 1)
    sibling = g + 1 - 2 * core
    across = (g + 8) % 16
    y, z = r // 8, r % 8
    y_mate = (1 - y) * 8 + z
    z_mate = y * 8 + (z + jnp.where((z + core) % 2 == 0, 1, 7)) % 8

    loads = [
        pltpu.make_async_copy(src, dst, loc.at[i])
        for i, (src, dst) in enumerate(
            (
                (feat, feat_v), (w_self_h, w_self), (cot_h, cot_v), (w_out_h, w_out),
                (w_agg_h, w_agg), (w_mid_h, w_mid),
                (tiles, tiles_t.at[pl.ds(f * 16, 16)]), (cols, cols_t.at[f]),
            )
        )
    ]
    for load in loads:
        load.start()
    greet([(g, wrap16(r + o)) for o in range(1, 16)] + [(wrap16(g + o), r) for o in range(1, 16)] + [(across, y_mate)])

    def slot(panel, rep):
        return win.at[pl.ds(panel * 32 + rep * 2, 2)]

    def source(row, d):
        return jnp.where(row == 0, y, 1 - y) * 8 + (z - d + 8) % 8

    def mate_copy():
        return remote(feat.at[:, :, lanes(1 - y, 256)], from_mate, s_mate, r_mate, g, y_mate)

    def chunk_copy(row, d, held=0):
        peer = y * 8 + (z - held + d) % 8
        if held:
            src = slot(1, source(row, held))
        else:
            src = (feat, from_mate)[row].at[:, :, lanes(quarter(peer) if row == 0 else peer % 2)]
        dst = slot(1, source(row, held))
        return remote(src, dst, s1.at[row, d], r1.at[row, d], g, peer)

    def chunk_arrival(row, d):
        view = slot(1, source(row, d))
        return remote(view, view, s1.at[row, d], r1.at[row, d], g, y * 8 + (z - d + 8) % 8)

    def ring_copies(row, d):
        src = source(row, d)
        return (
            remote(slot(1, src), slot(0, src), sx.at[row, d, 0], rx.at[row, d, 0], up, r),
            remote(slot(1, src), slot(2, src), sx.at[row, d, 1], rx.at[row, d, 1], down, r),
        )

    def ring_arrivals(row, d):
        src = source(row, d)
        return (
            remote(slot(0, src), slot(0, src), sx.at[row, d, 0], rx.at[row, d, 0], down, r),
            remote(slot(2, src), slot(2, src), sx.at[row, d, 1], rx.at[row, d, 1], up, r),
        )

    def send_ring(row, d):
        for copy in ring_copies(row, d):
            copy.start()

    def pass_on(row, d):
        chunk_arrival(row, d).wait_recv()
        if d in (1, 7):
            chunk_copy(row, 3 if d == 1 else 5, held=d).start()
        if d == (2 if row == 0 else 6):
            chunk_copy(row, 4, held=d).start()
        send_ring(row, d)

    def team(j):
        part = (f + j) % 4
        return part, mate(r, core, part)

    def cols_copy(j):
        return remote(cols, cols_t.at[f], sc.at[j], rc.at[j], g, team(j)[1])

    def cols_arrival(j):
        part, peer = team(4 - j)
        return remote(cols_t.at[part], cols_t.at[part], sc.at[j], rc.at[j], g, peer)

    def piece_of(rep, i):
        return tiles_t.at[pl.ds(quarter(rep) * 16 + i * 4, 4)]

    def tile_copy(way, i):
        peer = (y_mate, z_mate)[way]
        return remote(tiles.at[pl.ds(i * 4, 4)], piece_of(r, i), st.at[way, i], rt.at[way, i], g, peer)

    def tile_arrival(way, i):
        peer = (y_mate, z_mate)[way]
        return remote(piece_of(peer, i), piece_of(peer, i), st.at[way, i], rt.at[way, i], g, peer)

    def hand_copy(i):
        src, peer = (y_mate, z_mate) if i < HANDED_ALONG_Z else (z_mate, y_mate)
        return remote(piece_of(src, i), piece_of(src, i), st.at[2, i], rt.at[2, i], g, peer)

    def hand_arrival(i):
        far = mate(r, core, 3 - f)
        peer = z_mate if i < HANDED_ALONG_Z else y_mate
        return remote(piece_of(far, i), piece_of(far, i), st.at[2, i], rt.at[2, i], g, peer)

    for j in range(1, 4):
        cols_copy(j).start()

    mate_copy().start()
    for d in (1, 7, 2, 6):
        chunk_copy(0, d).start()
    for i in range(4):
        tile_copy(0, i).start()
    for i in range(HANDED_ALONG_Z, 4):
        tile_copy(1, i).start()
    own = pltpu.make_async_copy(feat.at[:, :, lanes(f)], slot(1, r), loc.at[8])
    own.start()
    own.wait()
    send_ring(0, 0)
    mate_copy().wait_recv()
    for d in (1, 7, 2, 6):
        chunk_copy(1, d).start()
    for i in range(HANDED_ALONG_Z):
        tile_copy(1, i).start()
    own = pltpu.make_async_copy(from_mate.at[:, :, lanes(z % 2)], slot(1, y_mate), loc.at[11])
    own.start()
    own.wait()
    send_ring(1, 0)
    for d in (1, 7, 2, 6):
        pass_on(0, d)
    for i in range(HANDED_ALONG_Z):
        tile_arrival(0, i).wait_recv()
        hand_copy(i).start()

    loads[7].wait()
    for j in range(1, 4):
        cols_arrival(j).wait_recv()
    to_smem = pltpu.make_async_copy(cols_t, cols_s, loc.at[9])
    to_smem.start()

    for i in range(4):
        loads[i].wait()
    feat2 = feat_v[...].reshape(256, 512)
    cot2 = cot_v[...]
    self_part[...] = dot(feat2, w_self[...])
    cot_part[...] = dot_bt(cot2, w_out[...])

    for d in (1, 7, 2, 6):
        pass_on(1, d)
    for i in range(HANDED_ALONG_Z, 4):
        tile_arrival(1, i).wait_recv()
        hand_copy(i).start()

    to_smem.wait()
    lane = lax.broadcasted_iota(jnp.int32, (8, 128), 1)
    start = jnp.zeros((8, 128), jnp.int32)
    slots = []
    for e in range(64):
        index = window_index(cols_s[e // 16, (e // 8) % 2, e % 8], g)
        slots.append(index)
        start = start + (index < lane).astype(jnp.int32)
        keys[e : e + 1, :] = jnp.full((1, 128), index * 64 + e, jnp.int32)
    all_keys = keys[...]
    rank = jnp.zeros((64, 128), jnp.int32)
    for e in range(64):
        rank = rank + (all_keys > slots[e] * 64 + e).astype(jnp.int32)
    lane64 = lax.broadcasted_iota(jnp.int32, (64, 128), 1)
    entry = lax.broadcasted_iota(jnp.int32, (64, 128), 0)
    order = jnp.sum(jnp.where(rank == lane64, entry, 0), axis=0, keepdims=True)
    table[0:8, :] = jnp.broadcast_to(order, (8, 128))
    table[8:16, :] = start
    to_smem = pltpu.make_async_copy(table, table_s, loc.at[10])
    to_smem.start()
    to_smem.wait()

    for d in (3, 5, 4):
        for row in range(2):
            pass_on(row, d)
    loads[6].wait()
    for i in range(HANDED_ALONG_Z, 4):
        tile_arrival(0, i).wait_recv()
    for i in range(HANDED_ALONG_Z):
        tile_arrival(1, i).wait_recv()
    for i in range(4):
        hand_arrival(i).wait_recv()
    for d in range(8):
        for row in range(2):
            for copy in ring_arrivals(row, d):
                copy.wait_recv()

    def agg_copy(j):
        part, peer = team(j)
        return remote(
            aggq.at[pl.ds(part * 2, 2)], aggr.at[:, :, lanes(f)], sa.at[j], ra.at[j], g, peer
        )

    def agg_arrival(j):
        part, peer = team(4 - j)
        view = aggr.at[:, :, lanes(part)]
        return remote(view, view, sa.at[j], ra.at[j], g, peer)

    def block_sum(part, half_of):
        picked = [win[window_index(cols_s[part, half_of, k], g)] for k in range(8)]
        left = jnp.concatenate([tiles_t[part * 16 + half_of * 8 + k] for k in range(8)], axis=1)
        return dot(left, jnp.concatenate(picked, axis=0)).astype(BF)

    for j in (1, 2, 3, 0):
        part = team(j)[0]
        for half_of in range(2):
            summed = block_sum(part, half_of)
            if j:
                aggq[part * 2 + half_of] = summed
            else:
                aggr[half_of, :, lanes(f)] = summed
        if j:
            agg_copy(j).start()
    loads[4].wait()
    loads[5].wait()
    for j in range(1, 4):
        agg_arrival(j).wait_recv()

    agg = aggr[...].reshape(256, 512)
    pre_first = dot(agg, w_agg[...]) + self_part[...]
    first = (pre_first * jax.nn.sigmoid(pre_first)).astype(BF)
    pre_second = dot(first, w_mid[...])
    second = (pre_second * jax.nn.sigmoid(pre_second)).astype(BF)
    delta_second = (cot_part[...] * silu_slope(pre_second)).astype(BF)
    delta_first = (dot_bt(delta_second, w_mid[...]) * silu_slope(pre_first)).astype(BF)
    dagg[...] = dot_bt(delta_first, w_agg[...]).astype(BF).reshape(2, 128, 512)

    def delta_copy(j):
        part, peer = team(j)
        return remote(
            dagg.at[:, :, lanes(part)], delt.at[pl.ds(f * 2, 2)], sd.at[j], rd.at[j], g, peer
        )

    def delta_arrival(j):
        part, peer = team(4 - j)
        view = delt.at[pl.ds(part * 2, 2)]
        return remote(view, view, sd.at[j], rd.at[j], g, peer)

    for j in range(1, 4):
        delta_copy(j).start()
    delt[pl.ds(f * 2, 2)] = dagg[:, :, lanes(f)]

    def core_copy(m):
        return remote(grads.at[m, :, lanes(1 - core, 256)], half_in.at[m], s_core.at[m], r_core.at[m], sibling, r)

    for m, (a, b) in enumerate(((second, cot2), (first, delta_second), (agg, delta_first), (feat2, delta_first))):
        grads[m] = dot_at(a, b).astype(BF)
        core_copy(m).start()
    upd[...] = (feat2.astype(F32) + dot(second, w_out[...])).astype(BF)
    base[...] = (cot2.astype(F32) + dot_bt(delta_first, w_self[...])).reshape(2, 128, 512)

    for m in range(4):
        core_copy(m).wait_recv()
        value = (grads[m, :, lanes(core, 256)].astype(F32) + half_in[m].astype(F32)).astype(BF)
        half[m] = value.reshape(16, 2, 16, 256)

    def y_peer(j):
        return across if j & 2 else g, y_mate if j & 1 else r

    def y_part(row, rep):
        return pl.ds((rep // 8) * 8, 8), lanes(row // 8)

    def x_peer(j):
        to = (x + j) % 4
        return y_hi * 8 + to * 2 + core, to

    def a_copy(j):
        row, rep = y_peer(j)
        rows, columns = y_part(row, rep)
        src = half.at[0:2, rows, :, :, columns]
        return remote(src, a_in.at[j - 1], s_a.at[j], r_a.at[j], row, rep)

    def b_copy(j):
        row, to = x_peer(j)
        src = half.at[2 + to // 2, :, to % 2]
        return remote(src, b_in.at[j - 1], s_b.at[j], r_b.at[j], row, r)

    def a2_copy(j):
        row, to = x_peer(j)
        return remote(a_sum.at[to // 2, :, to % 2], a2_in.at[j - 1], s_a2.at[j], r_a2.at[j], row, r)

    def b2_copy(j):
        row, rep = y_peer(j)
        rows, columns = y_part(row, rep)
        return remote(b_sum.at[rows, :, columns], b2_in.at[j - 1], s_b2.at[j], r_b2.at[j], row, rep)

    own_rows, own_columns = y_part(g, r)
    for j in range(1, 4):
        a_copy(j).start()
        b_copy(j).start()

    for j in range(1, 4):
        delta_arrival(j).wait_recv()

    csum[0] = jnp.zeros((128, 128), F32)

    def add_tiles(i, running):
        for step in range(4):
            e = table_s[0, i * 4 + step]
            running = running + dot_at(tiles_t[e], delt[lax.div(e, 8)])
            csum[i * 4 + step + 1] = running
        return running

    lax.fori_loop(0, 16, add_tiles, jnp.zeros((128, 128), F32))

    def message(w):
        return csum[table_s[8, w + 1]] - csum[table_s[8, w]]

    def message_copies(o):
        s = wrap16(r + o)
        rows = pl.ds(s * 2, 2)
        return (
            remote(to_prior.at[rows], from_next.at[rows], sm.at[0, o], rm.at[0, o], down, r),
            remote(to_next.at[rows], from_prior.at[rows], sm.at[1, o], rm.at[1, o], up, r),
        )

    def message_arrivals(o):
        s = wrap16(r + o)
        a = from_next.at[pl.ds(s * 2, 2)]
        b = from_prior.at[pl.ds(s * 2, 2)]
        return (
            remote(a, a, sm.at[0, o], rm.at[0, o], up, r),
            remote(b, b, sm.at[1, o], rm.at[1, o], down, r),
        )

    @pl.loop(0, 16)
    def _(i):
        o = lax.rem(i + 1, 16)
        s = wrap16(r + o)
        for part in range(2):
            to_prior[s * 2 + part] = message(s * 2 + part).astype(BF)
            to_next[s * 2 + part] = message(64 + s * 2 + part).astype(BF)
        for copy in message_copies(o):
            copy.start()

    def return_copy(o):
        s = wrap16(r + o)
        return remote(sums.at[pl.ds(s * 2, 2)], parts.at[pl.ds(r * 2, 2)], sp.at[o], rp.at[o], g, s)

    def return_arrival(o):
        s = wrap16(r - o)
        view = parts.at[pl.ds(s * 2, 2)]
        return remote(view, view, sp.at[o], rp.at[o], g, s)

    def total(s, part):
        i = s * 2 + part
        return (message(32 + i) + from_next[i].astype(F32) + from_prior[i].astype(F32)).astype(BF)

    def send_back(o):
        for copy in message_arrivals(o):
            copy.wait_recv()
        s = wrap16(r + o)
        for part in range(2):
            sums[s * 2 + part] = total(s, part)
        return_copy(o).start()

    pl.loop(1, Y_SUM_AT)(send_back)
    for j in range(1, 4):
        a_copy(j).wait_recv()
        b_copy(j).wait_recv()
    for m in range(2):
        value = half[m, own_rows, :, :, own_columns].astype(F32)
        for j in range(3):
            value = value + a_in[j, m].astype(F32)
        a_sum[m] = value.astype(BF)
    value = half[2 + x // 2, :, x % 2].astype(F32)
    for j in range(3):
        value = value + b_in[j].astype(F32)
    b_sum[...] = value.astype(BF)
    for j in range(1, 4):
        a2_copy(j).start()
        b2_copy(j).start()
    pl.loop(Y_SUM_AT, X_SUM_AT)(send_back)
    for j in range(1, 4):
        a2_copy(j).wait_recv()
        b2_copy(j).wait_recv()
    a_value = a_sum[x // 2, :, x % 2].astype(F32)
    b_value = b_sum[own_rows, :, own_columns].astype(F32)
    for j in range(3):
        a_value = a_value + a2_in[j].astype(F32)
        b_value = b_value + b2_in[j].astype(F32)
    last[:, 0] = a_value.astype(BF)
    last[:, 1] = b_value.astype(BF)

    def rep_copy(d):
        to = (z + d) % 8
        return remote(last.at[to], rep_in.at[d], s_rep.at[d], r_rep.at[d], g, y * 8 + to)

    for d in range(1, 8):
        rep_copy(d).start()
    pl.loop(X_SUM_AT, 16)(send_back)
    for copy in message_arrivals(0):
        copy.wait_recv()
    for part in range(2):
        parts[r * 2 + part] = total(r, part)

    acc = last[z].astype(F32)
    for d in range(1, 8):
        rep_copy(d).wait_recv()
        acc = acc + rep_in[d].astype(F32)
    piece[...] = acc * scale

    def place(row):
        to = (row // 2) % 4
        rows = pl.ds(pl.multiple_of((to % 2) * 16, 16), 16)
        return gout.at[:, to // 2, rows, lanes((row % 2) * 2 + row // 8)]

    def row_copy(o):
        return remote(piece, place(g), s_row.at[o], r_row.at[o], wrap16(g + o), r)

    def row_arrival(o):
        src = wrap16(g - o)
        return remote(piece, place(src), s_row.at[o], r_row.at[o], src, r)

    @pl.loop(1, 16)
    def _(o):
        row_copy(o).start()

    rows = pl.ds(pl.multiple_of((x % 2) * 16, 16), 16)
    gout[:, x // 2, rows, lanes(core * 2 + y_hi)] = piece[...]

    @pl.loop(1, 16)
    def _(o):
        return_arrival(o).wait_recv()

    for q in range(4):
        cut = slice(q * 128, q * 128 + 128)
        value = base[:, :, cut]
        for t in range(4):
            s = (q // 2) * 8 + 2 * t + q % 2
            value = value + parts[2 * s : 2 * s + 2].astype(F32)
        gf[:, :, cut] = value.astype(BF)

    @pl.loop(1, 16)
    def _(o):
        row_arrival(o).wait_recv()

    @pl.loop(0, 16)
    def _(o):
        for copy in message_copies(o):
            copy.wait_send()

    @pl.loop(1, 16)
    def _(o):
        return_copy(o).wait_send()
        row_copy(o).wait_send()

    mate_copy().wait_send()
    for row in range(2):
        for d in (1, 7, 2, 6):
            chunk_copy(row, d).wait_send()
        chunk_copy(row, 3, held=1).wait_send()
        chunk_copy(row, 5, held=7).wait_send()
        chunk_copy(row, 4, held=2 if row == 0 else 6).wait_send()
        for d in range(8):
            for copy in ring_copies(row, d):
                copy.wait_send()
    for i in range(4):
        tile_copy(0, i).wait_send()
        tile_copy(1, i).wait_send()
        hand_copy(i).wait_send()
    for m in range(4):
        core_copy(m).wait_send()
    for j in range(1, 4):
        a_copy(j).wait_send()
        b_copy(j).wait_send()
        a2_copy(j).wait_send()
        b2_copy(j).wait_send()
        cols_copy(j).wait_send()
        agg_copy(j).wait_send()
        delta_copy(j).wait_send()
    for d in range(1, 8):
        rep_copy(d).wait_send()


def shape(dims, kind):
    return jax.ShapeDtypeStruct(dims, kind)


def local(features, tiles, columns, w_aggregate, w_self, w_middle, w_output, cotangent):
    scale = 1.0 / math.sqrt(features.shape[0] * lax.axis_size("row") * lax.axis_size("rep"))
    weight = VMEM((512, 512), BF)
    panel = VMEM((32, 128, 128), BF)
    upd, gf, gout = pl.pallas_call(
        lambda *refs: layer_kernel(scale, *refs),
        out_shape=(shape((256, 512), BF), shape((2, 128, 512), BF), shape((2, 2, 32, 512), F32)),
        in_specs=[pl.BlockSpec(memory_space=pltpu.HBM)] * 8,
        out_specs=[pl.BlockSpec(memory_space=VMEM)] * 3,
        scratch_shapes=[
            VMEM((2, 128, 512), BF), VMEM((256, 512), BF), weight, weight, weight, weight,
            VMEM((64, 128, 128), BF), VMEM((4, 2, 8), jnp.int32), VMEM((96, 128, 128), BF),
            pltpu.SMEM((4, 2, 8), jnp.int32), VMEM((64, 128), jnp.int32),
            VMEM((16, 128), jnp.int32), pltpu.SMEM((16, 128), jnp.int32),
            VMEM((8, 128, 128), BF), VMEM((2, 128, 512), BF), VMEM((2, 128, 512), BF),
            VMEM((8, 128, 128), BF), VMEM((256, 512), F32), VMEM((256, 512), F32),
            VMEM((2, 128, 512), F32), VMEM((4, 512, 512), BF), VMEM((65, 128, 128), F32),
            panel, panel, panel, panel, panel, panel,
            VMEM((4, 512, 256), BF), VMEM((4, 16, 2, 16, 256), BF),
            VMEM((3, 2, 8, 2, 16, 128), BF), VMEM((3, 16, 16, 256), BF),
            VMEM((2, 8, 2, 16, 128), BF), VMEM((16, 16, 256), BF),
            VMEM((3, 8, 16, 128), BF), VMEM((3, 8, 16, 128), BF),
            VMEM((8, 2, 16, 128), BF), VMEM((8, 2, 16, 128), BF), VMEM((2, 16, 128), F32),
            VMEM((2, 128, 256), BF),
            DMA((12,)), DMA, DMA,
            DMA((2, 8)), DMA((2, 8)),
            DMA((2, 8, 2)), DMA((2, 8, 2)),
            DMA((3, 4)), DMA((3, 4)),
            DMA((4,)), DMA((4,)),
            DMA((4,)), DMA((4,)),
            DMA((4,)), DMA((4,)),
            DMA((2, 16)), DMA((2, 16)),
            DMA((16,)), DMA((16,)),
            DMA((4,)), DMA((4,)),
            DMA((4,)), DMA((4,)),
            DMA((4,)), DMA((4,)),
            DMA((4,)), DMA((4,)),
            DMA((4,)), DMA((4,)),
            DMA((8,)), DMA((8,)),
            DMA((16,)), DMA((16,)),
        ],
        compiler_params=pltpu.CompilerParams(
            collective_id=0, has_side_effects=True, vmem_limit_bytes=52 * 1024 * 1024
        ),
        name="message_passing_layer",
    )(
        *(
            pltpu.with_memory_space_constraint(value, pltpu.HBM)
            for value in (
                features.reshape(2, 128, 512), tiles.reshape(16, 128, 128), columns,
                w_aggregate, w_self, w_middle, w_output, cotangent,
            )
        )
    )
    return upd, gf.reshape(256, 512), gout[0, 0], gout[0, 1], gout[1, 0], gout[1, 1]


def solution(mesh):
    placed = (
        P(("row", "rep"), None),
        P(("row", "rep"), None, None, None),
        P(("row", "rep"), None),
        P(),
        P(),
        P(),
        P(),
        P(("row", "rep"), None),
    )
    return jax.shard_map(
        local,
        mesh=mesh,
        in_specs=placed,
        out_specs=(
            P(("row", "rep"), None),
            P(("row", "rep"), None),
            P("rep", None),
            P("rep", None),
            P("rep", None),
            P("rep", None),
        ),
        check_vma=False,
    )
```

```python
import math

import jax
import jax.numpy as jnp
from jax import lax
from jax.experimental import pallas as pl
from jax.experimental.pallas import tpu as pltpu
from jax.sharding import PartitionSpec as P

MESH = pl.DeviceIdType.MESH
BF = jnp.bfloat16
F32 = jnp.float32
VMEM = pltpu.VMEM
DMA = pltpu.SemaphoreType.DMA
HANDED_ALONG_Z = 2
Y_SUM_AT, X_SUM_AT = 13, 15


def wrap16(value):
    return lax.rem(value + 16, 16)


def quarter(rep):
    return (rep // 8) * 2 + rep % 2


def mate(rep, core, part):
    z = rep % 8
    step = jnp.where((z + core) % 2 == 0, 1, 7)
    other = (z + step) % 8
    return (part // 2) * 8 + jnp.where(z % 2 == part % 2, z, other)


def lanes(part, size=128):
    return pl.ds(pl.multiple_of(part * size, size), size)


def remote(src, dst, send, recv, row, rep):
    return pltpu.make_async_remote_copy(
        src_ref=src, dst_ref=dst, send_sem=send, recv_sem=recv, device_id=(row, rep), device_id_type=MESH
    )


def window_index(column, group):
    panel = jnp.minimum(lax.rem(lax.div(column, 32) - group + 17, 16), 2)
    return panel * 32 + lax.rem(column, 32)


def dot(a, b):
    return jnp.dot(a, b, preferred_element_type=F32)


def dot_bt(a, b):
    return lax.dot_general(a, b, (((1,), (1,)), ((), ())), preferred_element_type=F32)


def dot_at(a, b):
    return lax.dot_general(a, b, (((0,), (0,)), ((), ())), preferred_element_type=F32)


def silu_slope(value):
    sig = jax.nn.sigmoid(value)
    return sig * (1.0 + value * (1.0 - sig))


def greet(peers):
    barrier = pltpu.get_barrier_semaphore()
    for row, rep in peers:
        pl.semaphore_signal(barrier, inc=1, device_id=(row, rep), device_id_type=MESH)
    pl.semaphore_wait(barrier, len(peers))


def layer_kernel(
    scale,
    feat, tiles, cols, w_agg_h, w_self_h, w_mid_h, w_out_h, cot_h,
    upd, gf, gout,
    feat_v, cot_v, w_agg, w_self, w_mid, w_out,
    tiles_t, cols_t, win, cols_s, keys, table, table_s, aggq, aggr, dagg, delt, self_part, cot_part,
    base, grads, csum, to_next, to_prior, from_prior, from_next, sums, parts,
    half_in, half, a_in, b_in, a_sum, b_sum, a2_in, b2_in, last, rep_in, piece,
    from_mate, loc, s_mate, r_mate, s1, r1, sx, rx, st, rt, sc, rc, sa, ra, sd, rd,
    sm, rm, sp, rp, s_core, r_core, s_a, r_a, s_b, r_b, s_a2, r_a2, s_b2, r_b2, s_rep, r_rep, s_row, r_row,
):
    g = lax.axis_index("row")
    r = lax.axis_index("rep")
    core = g % 2
    x = (g // 2) % 4
    y_hi = g // 8
    f = quarter(r)
    up, down = wrap16(g + 1), wrap16(g - 1)
    sibling = g + 1 - 2 * core
    across = (g + 8) % 16
    y, z = r // 8, r % 8
    y_mate = (1 - y) * 8 + z
    z_mate = y * 8 + (z + jnp.where((z + core) % 2 == 0, 1, 7)) % 8

    loads = [
        pltpu.make_async_copy(src, dst, loc.at[i])
        for i, (src, dst) in enumerate(
            (
                (feat, feat_v), (w_self_h, w_self), (cot_h, cot_v), (w_out_h, w_out),
                (w_agg_h, w_agg), (w_mid_h, w_mid),
                (tiles, tiles_t.at[pl.ds(f * 16, 16)]), (cols, cols_t.at[f]),
            )
        )
    ]
    for load in loads:
        load.start()
    greet([(g, wrap16(r + o)) for o in range(1, 16)] + [(wrap16(g + o), r) for o in range(1, 16)] + [(across, y_mate)])

    def slot(panel, rep):
        return win.at[pl.ds(panel * 32 + rep * 2, 2)]

    def source(row, d):
        return jnp.where(row == 0, y, 1 - y) * 8 + (z - d + 8) % 8

    def mate_copy():
        return remote(feat.at[:, :, lanes(1 - y, 256)], from_mate, s_mate, r_mate, g, y_mate)

    def chunk_copy(row, d, held=0):
        peer = y * 8 + (z - held + d) % 8
        if held:
            src = slot(1, source(row, held))
        else:
            src = (feat, from_mate)[row].at[:, :, lanes(quarter(peer) if row == 0 else peer % 2)]
        dst = slot(1, source(row, held))
        return remote(src, dst, s1.at[row, d], r1.at[row, d], g, peer)

    def chunk_arrival(row, d):
        view = slot(1, source(row, d))
        return remote(view, view, s1.at[row, d], r1.at[row, d], g, y * 8 + (z - d + 8) % 8)

    def ring_copies(row, d):
        src = source(row, d)
        return (
            remote(slot(1, src), slot(0, src), sx.at[row, d, 0], rx.at[row, d, 0], up, r),
            remote(slot(1, src), slot(2, src), sx.at[row, d, 1], rx.at[row, d, 1], down, r),
        )

    def ring_arrivals(row, d):
        src = source(row, d)
        return (
            remote(slot(0, src), slot(0, src), sx.at[row, d, 0], rx.at[row, d, 0], down, r),
            remote(slot(2, src), slot(2, src), sx.at[row, d, 1], rx.at[row, d, 1], up, r),
        )

    def send_ring(row, d):
        for copy in ring_copies(row, d):
            copy.start()

    def pass_on(row, d):
        chunk_arrival(row, d).wait_recv()
        if d in (1, 7):
            chunk_copy(row, 3 if d == 1 else 5, held=d).start()
        if d == (2 if row == 0 else 6):
            chunk_copy(row, 4, held=d).start()
        send_ring(row, d)

    def team(j):
        part = (f + j) % 4
        return part, mate(r, core, part)

    def cols_copy(j):
        return remote(cols, cols_t.at[f], sc.at[j], rc.at[j], g, team(j)[1])

    def cols_arrival(j):
        part, peer = team(4 - j)
        return remote(cols_t.at[part], cols_t.at[part], sc.at[j], rc.at[j], g, peer)

    def piece_of(rep, i):
        return tiles_t.at[pl.ds(quarter(rep) * 16 + i * 4, 4)]

    def tile_copy(way, i):
        peer = (y_mate, z_mate)[way]
        return remote(tiles.at[pl.ds(i * 4, 4)], piece_of(r, i), st.at[way, i], rt.at[way, i], g, peer)

    def tile_arrival(way, i):
        peer = (y_mate, z_mate)[way]
        return remote(piece_of(peer, i), piece_of(peer, i), st.at[way, i], rt.at[way, i], g, peer)

    def hand_copy(i):
        src, peer = (y_mate, z_mate) if i < HANDED_ALONG_Z else (z_mate, y_mate)
        return remote(piece_of(src, i), piece_of(src, i), st.at[2, i], rt.at[2, i], g, peer)

    def hand_arrival(i):
        far = mate(r, core, 3 - f)
        peer = z_mate if i < HANDED_ALONG_Z else y_mate
        return remote(piece_of(far, i), piece_of(far, i), st.at[2, i], rt.at[2, i], g, peer)

    for j in range(1, 4):
        cols_copy(j).start()

    mate_copy().start()
    for d in (1, 7, 2, 6):
        chunk_copy(0, d).start()
    for i in range(4):
        tile_copy(0, i).start()
    for i in range(HANDED_ALONG_Z, 4):
        tile_copy(1, i).start()
    own = pltpu.make_async_copy(feat.at[:, :, lanes(f)], slot(1, r), loc.at[8])
    own.start()
    own.wait()
    send_ring(0, 0)
    mate_copy().wait_recv()
    for d in (1, 7, 2, 6):
        chunk_copy(1, d).start()
    for i in range(HANDED_ALONG_Z):
        tile_copy(1, i).start()
    own = pltpu.make_async_copy(from_mate.at[:, :, lanes(z % 2)], slot(1, y_mate), loc.at[11])
    own.start()
    own.wait()
    send_ring(1, 0)
    for d in (1, 7, 2, 6):
        pass_on(0, d)
    for i in range(HANDED_ALONG_Z):
        tile_arrival(0, i).wait_recv()
        hand_copy(i).start()

    loads[7].wait()
    for j in range(1, 4):
        cols_arrival(j).wait_recv()
    to_smem = pltpu.make_async_copy(cols_t, cols_s, loc.at[9])
    to_smem.start()

    for i in range(4):
        loads[i].wait()
    feat2 = feat_v[...].reshape(256, 512)
    cot2 = cot_v[...]
    self_part[...] = dot(feat2, w_self[...])
    cot_part[...] = dot_bt(cot2, w_out[...])

    for d in (1, 7, 2, 6):
        pass_on(1, d)
    for i in range(HANDED_ALONG_Z, 4):
        tile_arrival(1, i).wait_recv()
        hand_copy(i).start()

    to_smem.wait()
    lane = lax.broadcasted_iota(jnp.int32, (8, 128), 1)
    start = jnp.zeros((8, 128), jnp.int32)
    slots = []
    for e in range(64):
        index = window_index(cols_s[e // 16, (e // 8) % 2, e % 8], g)
        slots.append(index)
        start = start + (index < lane).astype(jnp.int32)
        keys[e : e + 1, :] = jnp.full((1, 128), index * 64 + e, jnp.int32)
    all_keys = keys[...]
    rank = jnp.zeros((64, 128), jnp.int32)
    for e in range(64):
        rank = rank + (all_keys > slots[e] * 64 + e).astype(jnp.int32)
    lane64 = lax.broadcasted_iota(jnp.int32, (64, 128), 1)
    entry = lax.broadcasted_iota(jnp.int32, (64, 128), 0)
    order = jnp.sum(jnp.where(rank == lane64, entry, 0), axis=0, keepdims=True)
    table[0:8, :] = jnp.broadcast_to(order, (8, 128))
    table[8:16, :] = start
    to_smem = pltpu.make_async_copy(table, table_s, loc.at[10])
    to_smem.start()
    to_smem.wait()

    for d in (3, 5, 4):
        for row in range(2):
            pass_on(row, d)
    loads[6].wait()
    for i in range(HANDED_ALONG_Z, 4):
        tile_arrival(0, i).wait_recv()
    for i in range(HANDED_ALONG_Z):
        tile_arrival(1, i).wait_recv()
    for i in range(4):
        hand_arrival(i).wait_recv()
    for d in range(8):
        for row in range(2):
            for copy in ring_arrivals(row, d):
                copy.wait_recv()

    def agg_copy(j):
        part, peer = team(j)
        return remote(
            aggq.at[pl.ds(part * 2, 2)], aggr.at[:, :, lanes(f)], sa.at[j], ra.at[j], g, peer
        )

    def agg_arrival(j):
        part, peer = team(4 - j)
        view = aggr.at[:, :, lanes(part)]
        return remote(view, view, sa.at[j], ra.at[j], g, peer)

    def block_sum(part, half_of):
        picked = [win[window_index(cols_s[part, half_of, k], g)] for k in range(8)]
        left = jnp.concatenate([tiles_t[part * 16 + half_of * 8 + k] for k in range(8)], axis=1)
        return dot(left, jnp.concatenate(picked, axis=0)).astype(BF)

    for j in (1, 2, 3, 0):
        part = team(j)[0]
        for half_of in range(2):
            summed = block_sum(part, half_of)
            if j:
                aggq[part * 2 + half_of] = summed
            else:
                aggr[half_of, :, lanes(f)] = summed
        if j:
            agg_copy(j).start()
    loads[4].wait()
    loads[5].wait()
    for j in range(1, 4):
        agg_arrival(j).wait_recv()

    agg = aggr[...].reshape(256, 512)
    pre_first = dot(agg, w_agg[...]) + self_part[...]
    first = (pre_first * jax.nn.sigmoid(pre_first)).astype(BF)
    pre_second = dot(first, w_mid[...])
    second = (pre_second * jax.nn.sigmoid(pre_second)).astype(BF)
    delta_second = (cot_part[...] * silu_slope(pre_second)).astype(BF)
    delta_first = (dot_bt(delta_second, w_mid[...]) * silu_slope(pre_first)).astype(BF)
    dagg[...] = dot_bt(delta_first, w_agg[...]).astype(BF).reshape(2, 128, 512)

    def delta_copy(j):
        part, peer = team(j)
        return remote(
            dagg.at[:, :, lanes(part)], delt.at[pl.ds(f * 2, 2)], sd.at[j], rd.at[j], g, peer
        )

    def delta_arrival(j):
        part, peer = team(4 - j)
        view = delt.at[pl.ds(part * 2, 2)]
        return remote(view, view, sd.at[j], rd.at[j], g, peer)

    for j in range(1, 4):
        delta_copy(j).start()
    delt[pl.ds(f * 2, 2)] = dagg[:, :, lanes(f)]

    def core_copy(m):
        return remote(grads.at[m, :, lanes(1 - core, 256)], half_in.at[m], s_core.at[m], r_core.at[m], sibling, r)

    for m, (a, b) in enumerate(((second, cot2), (first, delta_second), (agg, delta_first), (feat2, delta_first))):
        grads[m] = dot_at(a, b).astype(BF)
        core_copy(m).start()
    upd[...] = (feat2.astype(F32) + dot(second, w_out[...])).astype(BF)
    base[...] = (cot2.astype(F32) + dot_bt(delta_first, w_self[...])).reshape(2, 128, 512)

    for m in range(4):
        core_copy(m).wait_recv()
        value = (grads[m, :, lanes(core, 256)].astype(F32) + half_in[m].astype(F32)).astype(BF)
        half[m] = value.reshape(16, 2, 16, 256)

    def y_peer(j):
        return across if j & 2 else g, y_mate if j & 1 else r

    def y_part(row, rep):
        return pl.ds((rep // 8) * 8, 8), lanes(row // 8)

    def x_peer(j):
        to = (x + j) % 4
        return y_hi * 8 + to * 2 + core, to

    def a_copy(j):
        row, rep = y_peer(j)
        rows, columns = y_part(row, rep)
        src = half.at[0:2, rows, :, :, columns]
        return remote(src, a_in.at[j - 1], s_a.at[j], r_a.at[j], row, rep)

    def b_copy(j):
        row, to = x_peer(j)
        src = half.at[2 + to // 2, :, to % 2]
        return remote(src, b_in.at[j - 1], s_b.at[j], r_b.at[j], row, r)

    def a2_copy(j):
        row, to = x_peer(j)
        return remote(a_sum.at[to // 2, :, to % 2], a2_in.at[j - 1], s_a2.at[j], r_a2.at[j], row, r)

    def b2_copy(j):
        row, rep = y_peer(j)
        rows, columns = y_part(row, rep)
        return remote(b_sum.at[rows, :, columns], b2_in.at[j - 1], s_b2.at[j], r_b2.at[j], row, rep)

    own_rows, own_columns = y_part(g, r)
    for j in range(1, 4):
        a_copy(j).start()
        b_copy(j).start()

    for j in range(1, 4):
        delta_arrival(j).wait_recv()

    csum[0] = jnp.zeros((128, 128), F32)

    def add_tiles(i, running):
        for step in range(4):
            e = table_s[0, i * 4 + step]
            running = running + dot_at(tiles_t[e], delt[lax.div(e, 8)])
            csum[i * 4 + step + 1] = running
        return running

    lax.fori_loop(0, 16, add_tiles, jnp.zeros((128, 128), F32))

    def message(w):
        return csum[table_s[8, w + 1]] - csum[table_s[8, w]]

    def message_copies(o):
        s = wrap16(r + o)
        rows = pl.ds(s * 2, 2)
        return (
            remote(to_prior.at[rows], from_next.at[rows], sm.at[0, o], rm.at[0, o], down, r),
            remote(to_next.at[rows], from_prior.at[rows], sm.at[1, o], rm.at[1, o], up, r),
        )

    def message_arrivals(o):
        s = wrap16(r + o)
        a = from_next.at[pl.ds(s * 2, 2)]
        b = from_prior.at[pl.ds(s * 2, 2)]
        return (
            remote(a, a, sm.at[0, o], rm.at[0, o], up, r),
            remote(b, b, sm.at[1, o], rm.at[1, o], down, r),
        )

    @pl.loop(0, 16)
    def _(i):
        o = lax.rem(i + 1, 16)
        s = wrap16(r + o)
        for part in range(2):
            to_prior[s * 2 + part] = message(s * 2 + part).astype(BF)
            to_next[s * 2 + part] = message(64 + s * 2 + part).astype(BF)
        for copy in message_copies(o):
            copy.start()

    def return_copy(o):
        s = wrap16(r + o)
        return remote(sums.at[pl.ds(s * 2, 2)], parts.at[pl.ds(r * 2, 2)], sp.at[o], rp.at[o], g, s)

    def return_arrival(o):
        s = wrap16(r - o)
        view = parts.at[pl.ds(s * 2, 2)]
        return remote(view, view, sp.at[o], rp.at[o], g, s)

    def total(s, part):
        i = s * 2 + part
        return (message(32 + i) + from_next[i].astype(F32) + from_prior[i].astype(F32)).astype(BF)

    def send_back(o):
        for copy in message_arrivals(o):
            copy.wait_recv()
        s = wrap16(r + o)
        for part in range(2):
            sums[s * 2 + part] = total(s, part)
        return_copy(o).start()

    pl.loop(1, Y_SUM_AT)(send_back)
    for j in range(1, 4):
        a_copy(j).wait_recv()
        b_copy(j).wait_recv()
    for m in range(2):
        value = half[m, own_rows, :, :, own_columns].astype(F32)
        for j in range(3):
            value = value + a_in[j, m].astype(F32)
        a_sum[m] = value.astype(BF)
    value = half[2 + x // 2, :, x % 2].astype(F32)
    for j in range(3):
        value = value + b_in[j].astype(F32)
    b_sum[...] = value.astype(BF)
    for j in range(1, 4):
        a2_copy(j).start()
        b2_copy(j).start()
    pl.loop(Y_SUM_AT, X_SUM_AT)(send_back)
    for j in range(1, 4):
        a2_copy(j).wait_recv()
        b2_copy(j).wait_recv()
    a_value = a_sum[x // 2, :, x % 2].astype(F32)
    b_value = b_sum[own_rows, :, own_columns].astype(F32)
    for j in range(3):
        a_value = a_value + a2_in[j].astype(F32)
        b_value = b_value + b2_in[j].astype(F32)
    last[:, 0] = a_value.astype(BF)
    last[:, 1] = b_value.astype(BF)

    def rep_copy(d):
        to = (z + d) % 8
        return remote(last.at[to], rep_in.at[d], s_rep.at[d], r_rep.at[d], g, y * 8 + to)

    for d in range(1, 8):
        rep_copy(d).start()
    pl.loop(X_SUM_AT, 16)(send_back)
    for copy in message_arrivals(0):
        copy.wait_recv()
    for part in range(2):
        parts[r * 2 + part] = total(r, part)

    acc = last[z].astype(F32)
    for d in range(1, 8):
        rep_copy(d).wait_recv()
        acc = acc + rep_in[d].astype(F32)
    piece[...] = acc * scale

    def place(row):
        to = (row // 2) % 4
        rows = pl.ds(pl.multiple_of((to % 2) * 16, 16), 16)
        return gout.at[:, to // 2, rows, lanes((row % 2) * 2 + row // 8)]

    def row_copy(o):
        return remote(piece, place(g), s_row.at[o], r_row.at[o], wrap16(g + o), r)

    def row_arrival(o):
        src = wrap16(g - o)
        return remote(piece, place(src), s_row.at[o], r_row.at[o], src, r)

    @pl.loop(1, 16)
    def _(o):
        row_copy(o).start()

    rows = pl.ds(pl.multiple_of((x % 2) * 16, 16), 16)
    gout[:, x // 2, rows, lanes(core * 2 + y_hi)] = piece[...]

    @pl.loop(1, 16)
    def _(o):
        return_arrival(o).wait_recv()

    for q in range(4):
        cut = slice(q * 128, q * 128 + 128)
        value = base[:, :, cut]
        for t in range(4):
            s = (q // 2) * 8 + 2 * t + q % 2
            value = value + parts[2 * s : 2 * s + 2].astype(F32)
        gf[:, :, cut] = value.astype(BF)

    @pl.loop(1, 16)
    def _(o):
        row_arrival(o).wait_recv()

    @pl.loop(0, 16)
    def _(o):
        for copy in message_copies(o):
            copy.wait_send()

    @pl.loop(1, 16)
    def _(o):
        return_copy(o).wait_send()
        row_copy(o).wait_send()

    mate_copy().wait_send()
    for row in range(2):
        for d in (1, 7, 2, 6):
            chunk_copy(row, d).wait_send()
        chunk_copy(row, 3, held=1).wait_send()
        chunk_copy(row, 5, held=7).wait_send()
        chunk_copy(row, 4, held=2 if row == 0 else 6).wait_send()
        for d in range(8):
            for copy in ring_copies(row, d):
                copy.wait_send()
    for i in range(4):
        tile_copy(0, i).wait_send()
        tile_copy(1, i).wait_send()
        hand_copy(i).wait_send()
    for m in range(4):
        core_copy(m).wait_send()
    for j in range(1, 4):
        a_copy(j).wait_send()
        b_copy(j).wait_send()
        a2_copy(j).wait_send()
        b2_copy(j).wait_send()
        cols_copy(j).wait_send()
        agg_copy(j).wait_send()
        delta_copy(j).wait_send()
    for d in range(1, 8):
        rep_copy(d).wait_send()


def shape(dims, kind):
    return jax.ShapeDtypeStruct(dims, kind)


def local(features, tiles, columns, w_aggregate, w_self, w_middle, w_output, cotangent):
    scale = 1.0 / math.sqrt(features.shape[0] * lax.axis_size("row") * lax.axis_size("rep"))
    weight = VMEM((512, 512), BF)
    panel = VMEM((32, 128, 128), BF)
    upd, gf, gout = pl.pallas_call(
        lambda *refs: layer_kernel(scale, *refs),
        out_shape=(shape((256, 512), BF), shape((2, 128, 512), BF), shape((2, 2, 32, 512), F32)),
        in_specs=[pl.BlockSpec(memory_space=pltpu.HBM)] * 8,
        out_specs=[pl.BlockSpec(memory_space=VMEM)] * 3,
        scratch_shapes=[
            VMEM((2, 128, 512), BF), VMEM((256, 512), BF), weight, weight, weight, weight,
            VMEM((64, 128, 128), BF), VMEM((4, 2, 8), jnp.int32), VMEM((96, 128, 128), BF),
            pltpu.SMEM((4, 2, 8), jnp.int32), VMEM((64, 128), jnp.int32),
            VMEM((16, 128), jnp.int32), pltpu.SMEM((16, 128), jnp.int32),
            VMEM((8, 128, 128), BF), VMEM((2, 128, 512), BF), VMEM((2, 128, 512), BF),
            VMEM((8, 128, 128), BF), VMEM((256, 512), F32), VMEM((256, 512), F32),
            VMEM((2, 128, 512), F32), VMEM((4, 512, 512), BF), VMEM((65, 128, 128), F32),
            panel, panel, panel, panel, panel, panel,
            VMEM((4, 512, 256), BF), VMEM((4, 16, 2, 16, 256), BF),
            VMEM((3, 2, 8, 2, 16, 128), BF), VMEM((3, 16, 16, 256), BF),
            VMEM((2, 8, 2, 16, 128), BF), VMEM((16, 16, 256), BF),
            VMEM((3, 8, 16, 128), BF), VMEM((3, 8, 16, 128), BF),
            VMEM((8, 2, 16, 128), BF), VMEM((8, 2, 16, 128), BF), VMEM((2, 16, 128), F32),
            VMEM((2, 128, 256), BF),
            DMA((12,)), DMA, DMA,
            DMA((2, 8)), DMA((2, 8)),
            DMA((2, 8, 2)), DMA((2, 8, 2)),
            DMA((3, 4)), DMA((3, 4)),
            DMA((4,)), DMA((4,)),
            DMA((4,)), DMA((4,)),
            DMA((4,)), DMA((4,)),
            DMA((2, 16)), DMA((2, 16)),
            DMA((16,)), DMA((16,)),
            DMA((4,)), DMA((4,)),
            DMA((4,)), DMA((4,)),
            DMA((4,)), DMA((4,)),
            DMA((4,)), DMA((4,)),
            DMA((4,)), DMA((4,)),
            DMA((8,)), DMA((8,)),
            DMA((16,)), DMA((16,)),
        ],
        compiler_params=pltpu.CompilerParams(
            collective_id=0, has_side_effects=True, vmem_limit_bytes=52 * 1024 * 1024
        ),
        name="message_passing_layer",
    )(
        *(
            pltpu.with_memory_space_constraint(value, pltpu.HBM)
            for value in (
                features.reshape(2, 128, 512), tiles.reshape(16, 128, 128), columns,
                w_aggregate, w_self, w_middle, w_output, cotangent,
            )
        )
    )
    return upd, gf.reshape(256, 512), gout[0, 0], gout[0, 1], gout[1, 0], gout[1, 1]


def solution(mesh):
    placed = (
        P(("row", "rep"), None),
        P(("row", "rep"), None, None, None),
        P(("row", "rep"), None),
        P(),
        P(),
        P(),
        P(),
        P(("row", "rep"), None),
    )
    return jax.shard_map(
        local,
        mesh=mesh,
        in_specs=placed,
        out_specs=(
            P(("row", "rep"), None),
            P(("row", "rep"), None),
            P("rep", None),
            P("rep", None),
            P("rep", None),
            P("rep", None),
        ),
        check_vma=False,
    )
```

```python
import math

import jax
import jax.numpy as jnp
from jax import lax
from jax.experimental import pallas as pl
from jax.experimental.pallas import tpu as pltpu
from jax.sharding import PartitionSpec as P

MESH = pl.DeviceIdType.MESH
BF = jnp.bfloat16
F32 = jnp.float32
VMEM = pltpu.VMEM
DMA = pltpu.SemaphoreType.DMA
HANDED_ALONG_Z = 2
Y_SUM_AT, X_SUM_AT = 11, 14


def wrap16(value):
    return lax.rem(value + 16, 16)


def quarter(rep):
    return (rep // 8) * 2 + rep % 2


def mate(rep, core, part):
    z = rep % 8
    step = jnp.where((z + core) % 2 == 0, 1, 7)
    other = (z + step) % 8
    return (part // 2) * 8 + jnp.where(z % 2 == part % 2, z, other)


def lanes(part, size=128):
    return pl.ds(pl.multiple_of(part * size, size), size)


def remote(src, dst, send, recv, row, rep):
    return pltpu.make_async_remote_copy(
        src_ref=src, dst_ref=dst, send_sem=send, recv_sem=recv, device_id=(row, rep), device_id_type=MESH
    )


def window_index(column, group):
    panel = jnp.minimum(lax.rem(lax.div(column, 32) - group + 17, 16), 2)
    return panel * 32 + lax.rem(column, 32)


def dot(a, b):
    return jnp.dot(a, b, preferred_element_type=F32)


def dot_bt(a, b):
    return lax.dot_general(a, b, (((1,), (1,)), ((), ())), preferred_element_type=F32)


def dot_at(a, b):
    return lax.dot_general(a, b, (((0,), (0,)), ((), ())), preferred_element_type=F32)


def silu_slope(value):
    sig = jax.nn.sigmoid(value)
    return sig * (1.0 + value * (1.0 - sig))


def greet(peers):
    barrier = pltpu.get_barrier_semaphore()
    for row, rep in peers:
        pl.semaphore_signal(barrier, inc=1, device_id=(row, rep), device_id_type=MESH)
    pl.semaphore_wait(barrier, len(peers))


def layer_kernel(
    scale,
    feat, tiles, cols, w_agg_h, w_self_h, w_mid_h, w_out_h, cot_h,
    upd, gf, gout,
    feat_v, cot_v, w_agg, w_self, w_mid, w_out,
    tiles_t, cols_t, win, cols_s, keys, table, table_s, aggq, aggr, dagg, delt, self_part, cot_part,
    base, grads, csum, to_next, to_prior, from_prior, from_next, sums, parts,
    half_in, half, a_in, b_in, a_sum, b_sum, a2_in, b2_in, last, rep_in, piece,
    from_mate, delt_t, loc, s_mate, r_mate, s1, r1, sx, rx, st, rt, sc, rc, sa, ra, sd, rd,
    sm, rm, sp, rp, s_core, r_core, s_a, r_a, s_b, r_b, s_a2, r_a2, s_b2, r_b2, s_rep, r_rep, s_row, r_row,
):
    g = lax.axis_index("row")
    r = lax.axis_index("rep")
    core = g % 2
    x = (g // 2) % 4
    y_hi = g // 8
    f = quarter(r)
    up, down = wrap16(g + 1), wrap16(g - 1)
    sibling = g + 1 - 2 * core
    across = (g + 8) % 16
    y, z = r // 8, r % 8
    y_mate = (1 - y) * 8 + z
    z_mate = y * 8 + (z + jnp.where((z + core) % 2 == 0, 1, 7)) % 8

    loads = [
        pltpu.make_async_copy(src, dst, loc.at[i])
        for i, (src, dst) in enumerate(
            (
                (feat, feat_v), (w_self_h, w_self), (cot_h, cot_v), (w_out_h, w_out),
                (w_agg_h, w_agg), (w_mid_h, w_mid),
                (tiles, tiles_t.at[pl.ds(f * 16, 16)]), (cols, cols_t.at[f]),
            )
        )
    ]
    for load in loads:
        load.start()
    greet([(g, wrap16(r + o)) for o in range(1, 16)] + [(wrap16(g + o), r) for o in range(1, 16)] + [(across, y_mate)])

    def slot(panel, rep):
        return win.at[pl.ds(panel * 32 + rep * 2, 2)]

    def source(row, d):
        return jnp.where(row == 0, y, 1 - y) * 8 + (z - d + 8) % 8

    def mate_copy():
        return remote(feat.at[:, :, lanes(1 - y, 256)], from_mate, s_mate, r_mate, g, y_mate)

    def chunk_copy(row, d, held=0):
        peer = y * 8 + (z - held + d) % 8
        if held:
            src = slot(1, source(row, held))
        else:
            src = (feat, from_mate)[row].at[:, :, lanes(quarter(peer) if row == 0 else peer % 2)]
        dst = slot(1, source(row, held))
        return remote(src, dst, s1.at[row, d], r1.at[row, d], g, peer)

    def chunk_arrival(row, d):
        view = slot(1, source(row, d))
        return remote(view, view, s1.at[row, d], r1.at[row, d], g, y * 8 + (z - d + 8) % 8)

    def ring_copies(row, d):
        src = source(row, d)
        return (
            remote(slot(1, src), slot(0, src), sx.at[row, d, 0], rx.at[row, d, 0], up, r),
            remote(slot(1, src), slot(2, src), sx.at[row, d, 1], rx.at[row, d, 1], down, r),
        )

    def ring_arrivals(row, d):
        src = source(row, d)
        return (
            remote(slot(0, src), slot(0, src), sx.at[row, d, 0], rx.at[row, d, 0], down, r),
            remote(slot(2, src), slot(2, src), sx.at[row, d, 1], rx.at[row, d, 1], up, r),
        )

    def send_ring(row, d):
        for copy in ring_copies(row, d):
            copy.start()

    def pass_on(row, d):
        chunk_arrival(row, d).wait_recv()
        if d in (1, 7):
            chunk_copy(row, 3 if d == 1 else 5, held=d).start()
        if d == (2 if row == 0 else 6):
            chunk_copy(row, 4, held=d).start()
        send_ring(row, d)

    def team(j):
        part = (f + j) % 4
        return part, mate(r, core, part)

    def cols_copy(j):
        return remote(cols, cols_t.at[f], sc.at[j], rc.at[j], g, team(j)[1])

    def cols_arrival(j):
        part, peer = team(4 - j)
        return remote(cols_t.at[part], cols_t.at[part], sc.at[j], rc.at[j], g, peer)

    def piece_of(rep, i):
        return tiles_t.at[pl.ds(quarter(rep) * 16 + i * 4, 4)]

    def tile_copy(way, i):
        peer = (y_mate, z_mate)[way]
        return remote(tiles.at[pl.ds(i * 4, 4)], piece_of(r, i), st.at[way, i], rt.at[way, i], g, peer)

    def tile_arrival(way, i):
        peer = (y_mate, z_mate)[way]
        return remote(piece_of(peer, i), piece_of(peer, i), st.at[way, i], rt.at[way, i], g, peer)

    def hand_copy(i):
        src, peer = (y_mate, z_mate) if i < HANDED_ALONG_Z else (z_mate, y_mate)
        return remote(piece_of(src, i), piece_of(src, i), st.at[2, i], rt.at[2, i], g, peer)

    def hand_arrival(i):
        far = mate(r, core, 3 - f)
        peer = z_mate if i < HANDED_ALONG_Z else y_mate
        return remote(piece_of(far, i), piece_of(far, i), st.at[2, i], rt.at[2, i], g, peer)

    for j in range(1, 4):
        cols_copy(j).start()

    mate_copy().start()
    for d in (1, 7, 2, 6):
        chunk_copy(0, d).start()
    for i in range(4):
        tile_copy(0, i).start()
    for i in range(HANDED_ALONG_Z, 4):
        tile_copy(1, i).start()
    own = pltpu.make_async_copy(feat.at[:, :, lanes(f)], slot(1, r), loc.at[8])
    own.start()
    own.wait()
    send_ring(0, 0)
    mate_copy().wait_recv()
    for d in (1, 7, 2, 6):
        chunk_copy(1, d).start()
    for i in range(HANDED_ALONG_Z):
        tile_copy(1, i).start()
    own = pltpu.make_async_copy(from_mate.at[:, :, lanes(z % 2)], slot(1, y_mate), loc.at[11])
    own.start()
    own.wait()
    send_ring(1, 0)
    for d in (1, 7, 2, 6):
        pass_on(0, d)
    for i in range(HANDED_ALONG_Z):
        tile_arrival(0, i).wait_recv()
        hand_copy(i).start()

    loads[7].wait()
    for j in range(1, 4):
        cols_arrival(j).wait_recv()
    to_smem = pltpu.make_async_copy(cols_t, cols_s, loc.at[9])
    to_smem.start()

    for i in range(4):
        loads[i].wait()
    feat2 = feat_v[...].reshape(256, 512)
    cot2 = cot_v[...]
    self_part[...] = dot(feat2, w_self[...])
    cot_part[...] = dot_bt(cot2, w_out[...])

    for d in (1, 7, 2, 6):
        pass_on(1, d)
    for i in range(HANDED_ALONG_Z, 4):
        tile_arrival(1, i).wait_recv()
        hand_copy(i).start()

    to_smem.wait()
    lane = lax.broadcasted_iota(jnp.int32, (8, 128), 1)
    start = jnp.zeros((8, 128), jnp.int32)
    slots = []
    for e in range(64):
        index = window_index(cols_s[e // 16, (e // 8) % 2, e % 8], g)
        slots.append(index)
        start = start + (index < lane).astype(jnp.int32)
        keys[e : e + 1, :] = jnp.full((1, 128), index * 64 + e, jnp.int32)
    all_keys = keys[...]
    rank = jnp.zeros((64, 128), jnp.int32)
    for e in range(64):
        rank = rank + (all_keys > slots[e] * 64 + e).astype(jnp.int32)
    lane64 = lax.broadcasted_iota(jnp.int32, (64, 128), 1)
    entry = lax.broadcasted_iota(jnp.int32, (64, 128), 0)
    order = jnp.sum(jnp.where(rank == lane64, entry, 0), axis=0, keepdims=True)
    table[0:8, :] = jnp.broadcast_to(order, (8, 128))
    table[8:16, :] = start
    to_smem = pltpu.make_async_copy(table, table_s, loc.at[10])
    to_smem.start()
    to_smem.wait()

    for d in (3, 5, 4):
        for row in range(2):
            pass_on(row, d)
    loads[6].wait()
    for i in range(HANDED_ALONG_Z, 4):
        tile_arrival(0, i).wait_recv()
    for i in range(HANDED_ALONG_Z):
        tile_arrival(1, i).wait_recv()
    for i in range(4):
        hand_arrival(i).wait_recv()
    for d in range(8):
        for row in range(2):
            for copy in ring_arrivals(row, d):
                copy.wait_recv()

    def agg_copy(j):
        part, peer = team(j)
        return remote(
            aggq.at[pl.ds(part * 2, 2)], aggr.at[:, :, lanes(f)], sa.at[j], ra.at[j], g, peer
        )

    def agg_arrival(j):
        part, peer = team(4 - j)
        view = aggr.at[:, :, lanes(part)]
        return remote(view, view, sa.at[j], ra.at[j], g, peer)

    def block_sum(part, half_of):
        picked = [win[window_index(cols_s[part, half_of, k], g)] for k in range(8)]
        left = jnp.concatenate([tiles_t[part * 16 + half_of * 8 + k] for k in range(8)], axis=1)
        return dot(left, jnp.concatenate(picked, axis=0)).astype(BF)

    for j in (1, 2, 3, 0):
        part = team(j)[0]
        for half_of in range(2):
            summed = block_sum(part, half_of)
            if j:
                aggq[part * 2 + half_of] = summed
            else:
                aggr[half_of, :, lanes(f)] = summed
        if j:
            agg_copy(j).start()
    loads[4].wait()
    loads[5].wait()
    for j in range(1, 4):
        agg_arrival(j).wait_recv()

    agg = aggr[...].reshape(256, 512)
    pre_first = dot(agg, w_agg[...]) + self_part[...]
    first = (pre_first * jax.nn.sigmoid(pre_first)).astype(BF)
    pre_second = dot(first, w_mid[...])
    second = (pre_second * jax.nn.sigmoid(pre_second)).astype(BF)
    delta_second = (cot_part[...] * silu_slope(pre_second)).astype(BF)
    delta_first = (dot_bt(delta_second, w_mid[...]) * silu_slope(pre_first)).astype(BF)
    dagg[...] = dot_bt(delta_first, w_agg[...]).astype(BF).reshape(2, 128, 512)

    def delta_copy(j):
        part, peer = team(j)
        return remote(
            dagg.at[:, :, lanes(part)], delt.at[pl.ds(f * 2, 2)], sd.at[j], rd.at[j], g, peer
        )

    def delta_arrival(j):
        part, peer = team(4 - j)
        view = delt.at[pl.ds(part * 2, 2)]
        return remote(view, view, sd.at[j], rd.at[j], g, peer)

    for j in range(1, 4):
        delta_copy(j).start()
    delt[pl.ds(f * 2, 2)] = dagg[:, :, lanes(f)]

    def core_copy(m):
        return remote(grads.at[m, :, lanes(1 - core, 256)], half_in.at[m], s_core.at[m], r_core.at[m], sibling, r)

    for m, (a, b) in enumerate(((second, cot2), (first, delta_second), (agg, delta_first), (feat2, delta_first))):
        grads[m] = dot_at(a, b).astype(BF)
        core_copy(m).start()
    upd[...] = (feat2.astype(F32) + dot(second, w_out[...])).astype(BF)
    base[...] = (cot2.astype(F32) + dot_bt(delta_first, w_self[...])).reshape(2, 128, 512)

    for m in range(4):
        core_copy(m).wait_recv()
        value = (grads[m, :, lanes(core, 256)].astype(F32) + half_in[m].astype(F32)).astype(BF)
        half[m] = value.reshape(16, 2, 16, 256)

    def y_peer(j):
        return across if j & 2 else g, y_mate if j & 1 else r

    def y_part(row, rep):
        return pl.ds((rep // 8) * 8, 8), lanes(row // 8)

    def x_peer(j):
        to = (x + j) % 4
        return y_hi * 8 + to * 2 + core, to

    def a_copy(j):
        row, rep = y_peer(j)
        rows, columns = y_part(row, rep)
        src = half.at[0:2, rows, :, :, columns]
        return remote(src, a_in.at[j - 1], s_a.at[j], r_a.at[j], row, rep)

    def b_copy(j):
        row, to = x_peer(j)
        src = half.at[2 + to // 2, :, to % 2]
        return remote(src, b_in.at[j - 1], s_b.at[j], r_b.at[j], row, r)

    def a2_copy(j):
        row, to = x_peer(j)
        return remote(a_sum.at[to // 2, :, to % 2], a2_in.at[j - 1], s_a2.at[j], r_a2.at[j], row, r)

    def b2_copy(j):
        row, rep = y_peer(j)
        rows, columns = y_part(row, rep)
        return remote(b_sum.at[rows, :, columns], b2_in.at[j - 1], s_b2.at[j], r_b2.at[j], row, rep)

    own_rows, own_columns = y_part(g, r)
    for j in range(1, 4):
        a_copy(j).start()
        b_copy(j).start()

    for j in range(1, 4):
        delta_arrival(j).wait_recv()

    for i in range(8):
        delt_t[i] = delt[i].T
    csum[0] = jnp.zeros((128, 128), F32)

    def add_tiles(i, running):
        for step in range(4):
            e = table_s[0, i * 4 + step]
            running = running + dot(delt_t[lax.div(e, 8)], tiles_t[e])
            csum[i * 4 + step + 1] = running
        return running

    lax.fori_loop(0, 16, add_tiles, jnp.zeros((128, 128), F32))

    def message(w):
        return csum[table_s[8, w + 1]] - csum[table_s[8, w]]

    def message_copies(o):
        s = wrap16(r + o)
        rows = pl.ds(s * 2, 2)
        return (
            remote(to_prior.at[rows], from_next.at[rows], sm.at[0, o], rm.at[0, o], down, r),
            remote(to_next.at[rows], from_prior.at[rows], sm.at[1, o], rm.at[1, o], up, r),
        )

    def message_arrivals(o):
        s = wrap16(r + o)
        a = from_next.at[pl.ds(s * 2, 2)]
        b = from_prior.at[pl.ds(s * 2, 2)]
        return (
            remote(a, a, sm.at[0, o], rm.at[0, o], up, r),
            remote(b, b, sm.at[1, o], rm.at[1, o], down, r),
        )

    @pl.loop(0, 16)
    def _(i):
        o = lax.rem(i + 1, 16)
        s = wrap16(r + o)
        for part in range(2):
            to_prior[s * 2 + part] = message(s * 2 + part).astype(BF)
            to_next[s * 2 + part] = message(64 + s * 2 + part).astype(BF)
        for copy in message_copies(o):
            copy.start()

    def return_copy(o):
        s = wrap16(r + o)
        return remote(sums.at[pl.ds(s * 2, 2)], parts.at[pl.ds(r * 2, 2)], sp.at[o], rp.at[o], g, s)

    def return_arrival(o):
        s = wrap16(r - o)
        view = parts.at[pl.ds(s * 2, 2)]
        return remote(view, view, sp.at[o], rp.at[o], g, s)

    def total(s, part):
        i = s * 2 + part
        return (message(32 + i) + from_next[i].astype(F32) + from_prior[i].astype(F32)).astype(BF)

    def send_back(o):
        for copy in message_arrivals(o):
            copy.wait_recv()
        s = wrap16(r + o)
        for part in range(2):
            sums[s * 2 + part] = total(s, part)
        return_copy(o).start()

    pl.loop(1, Y_SUM_AT)(send_back)
    for j in range(1, 4):
        a_copy(j).wait_recv()
        b_copy(j).wait_recv()
    for m in range(2):
        value = half[m, own_rows, :, :, own_columns].astype(F32)
        for j in range(3):
            value = value + a_in[j, m].astype(F32)
        a_sum[m] = value.astype(BF)
    value = half[2 + x // 2, :, x % 2].astype(F32)
    for j in range(3):
        value = value + b_in[j].astype(F32)
    b_sum[...] = value.astype(BF)
    for j in range(1, 4):
        a2_copy(j).start()
        b2_copy(j).start()
    pl.loop(Y_SUM_AT, X_SUM_AT)(send_back)
    for j in range(1, 4):
        a2_copy(j).wait_recv()
        b2_copy(j).wait_recv()
    a_value = a_sum[x // 2, :, x % 2].astype(F32)
    b_value = b_sum[own_rows, :, own_columns].astype(F32)
    for j in range(3):
        a_value = a_value + a2_in[j].astype(F32)
        b_value = b_value + b2_in[j].astype(F32)
    last[:, 0] = a_value.astype(BF)
    last[:, 1] = b_value.astype(BF)

    def rep_copy(d):
        to = (z + d) % 8
        return remote(last.at[to], rep_in.at[d], s_rep.at[d], r_rep.at[d], g, y * 8 + to)

    for d in range(1, 8):
        rep_copy(d).start()
    pl.loop(X_SUM_AT, 16)(send_back)
    for copy in message_arrivals(0):
        copy.wait_recv()
    for part in range(2):
        parts[r * 2 + part] = total(r, part)

    acc = last[z].astype(F32)
    for d in range(1, 8):
        rep_copy(d).wait_recv()
        acc = acc + rep_in[d].astype(F32)
    piece[...] = acc * scale

    def place(row):
        to = (row // 2) % 4
        rows = pl.ds(pl.multiple_of((to % 2) * 16, 16), 16)
        return gout.at[:, to // 2, rows, lanes((row % 2) * 2 + row // 8)]

    def row_copy(o):
        return remote(piece, place(g), s_row.at[o], r_row.at[o], wrap16(g + o), r)

    def row_arrival(o):
        src = wrap16(g - o)
        return remote(piece, place(src), s_row.at[o], r_row.at[o], src, r)

    @pl.loop(1, 16)
    def _(o):
        row_copy(o).start()

    rows = pl.ds(pl.multiple_of((x % 2) * 16, 16), 16)
    gout[:, x // 2, rows, lanes(core * 2 + y_hi)] = piece[...]

    @pl.loop(1, 16)
    def _(o):
        return_arrival(o).wait_recv()

    for q in range(4):
        cut = slice(q * 128, q * 128 + 128)
        for half_of in range(2):
            value = jnp.zeros((128, 128), F32)
            for t in range(4):
                s = (q // 2) * 8 + 2 * t + q % 2
                value = value + parts[2 * s + half_of].astype(F32)
            gf[half_of, :, cut] = (base[half_of, :, cut] + value.T).astype(BF)

    @pl.loop(1, 16)
    def _(o):
        row_arrival(o).wait_recv()

    @pl.loop(0, 16)
    def _(o):
        for copy in message_copies(o):
            copy.wait_send()

    @pl.loop(1, 16)
    def _(o):
        return_copy(o).wait_send()
        row_copy(o).wait_send()

    mate_copy().wait_send()
    for row in range(2):
        for d in (1, 7, 2, 6):
            chunk_copy(row, d).wait_send()
        chunk_copy(row, 3, held=1).wait_send()
        chunk_copy(row, 5, held=7).wait_send()
        chunk_copy(row, 4, held=2 if row == 0 else 6).wait_send()
        for d in range(8):
            for copy in ring_copies(row, d):
                copy.wait_send()
    for i in range(4):
        tile_copy(0, i).wait_send()
        tile_copy(1, i).wait_send()
        hand_copy(i).wait_send()
    for m in range(4):
        core_copy(m).wait_send()
    for j in range(1, 4):
        a_copy(j).wait_send()
        b_copy(j).wait_send()
        a2_copy(j).wait_send()
        b2_copy(j).wait_send()
        cols_copy(j).wait_send()
        agg_copy(j).wait_send()
        delta_copy(j).wait_send()
    for d in range(1, 8):
        rep_copy(d).wait_send()


def shape(dims, kind):
    return jax.ShapeDtypeStruct(dims, kind)


def local(features, tiles, columns, w_aggregate, w_self, w_middle, w_output, cotangent):
    scale = 1.0 / math.sqrt(features.shape[0] * lax.axis_size("row") * lax.axis_size("rep"))
    weight = VMEM((512, 512), BF)
    panel = VMEM((32, 128, 128), BF)
    upd, gf, gout = pl.pallas_call(
        lambda *refs: layer_kernel(scale, *refs),
        out_shape=(shape((256, 512), BF), shape((2, 128, 512), BF), shape((2, 2, 32, 512), F32)),
        in_specs=[pl.BlockSpec(memory_space=pltpu.HBM)] * 8,
        out_specs=[pl.BlockSpec(memory_space=VMEM)] * 3,
        scratch_shapes=[
            VMEM((2, 128, 512), BF), VMEM((256, 512), BF), weight, weight, weight, weight,
            VMEM((64, 128, 128), BF), VMEM((4, 2, 8), jnp.int32), VMEM((96, 128, 128), BF),
            pltpu.SMEM((4, 2, 8), jnp.int32), VMEM((64, 128), jnp.int32),
            VMEM((16, 128), jnp.int32), pltpu.SMEM((16, 128), jnp.int32),
            VMEM((8, 128, 128), BF), VMEM((2, 128, 512), BF), VMEM((2, 128, 512), BF),
            VMEM((8, 128, 128), BF), VMEM((256, 512), F32), VMEM((256, 512), F32),
            VMEM((2, 128, 512), F32), VMEM((4, 512, 512), BF), VMEM((65, 128, 128), F32),
            panel, panel, panel, panel, panel, panel,
            VMEM((4, 512, 256), BF), VMEM((4, 16, 2, 16, 256), BF),
            VMEM((3, 2, 8, 2, 16, 128), BF), VMEM((3, 16, 16, 256), BF),
            VMEM((2, 8, 2, 16, 128), BF), VMEM((16, 16, 256), BF),
            VMEM((3, 8, 16, 128), BF), VMEM((3, 8, 16, 128), BF),
            VMEM((8, 2, 16, 128), BF), VMEM((8, 2, 16, 128), BF), VMEM((2, 16, 128), F32),
            VMEM((2, 128, 256), BF), VMEM((8, 128, 128), BF),
            DMA((12,)), DMA, DMA,
            DMA((2, 8)), DMA((2, 8)),
            DMA((2, 8, 2)), DMA((2, 8, 2)),
            DMA((3, 4)), DMA((3, 4)),
            DMA((4,)), DMA((4,)),
            DMA((4,)), DMA((4,)),
            DMA((4,)), DMA((4,)),
            DMA((2, 16)), DMA((2, 16)),
            DMA((16,)), DMA((16,)),
            DMA((4,)), DMA((4,)),
            DMA((4,)), DMA((4,)),
            DMA((4,)), DMA((4,)),
            DMA((4,)), DMA((4,)),
            DMA((4,)), DMA((4,)),
            DMA((8,)), DMA((8,)),
            DMA((16,)), DMA((16,)),
        ],
        compiler_params=pltpu.CompilerParams(
            collective_id=0, has_side_effects=True, vmem_limit_bytes=52 * 1024 * 1024
        ),
        name="message_passing_layer",
    )(
        *(
            pltpu.with_memory_space_constraint(value, pltpu.HBM)
            for value in (
                features.reshape(2, 128, 512), tiles.reshape(16, 128, 128), columns,
                w_aggregate, w_self, w_middle, w_output, cotangent,
            )
        )
    )
    return upd, gf.reshape(256, 512), gout[0, 0], gout[0, 1], gout[1, 0], gout[1, 1]


def solution(mesh):
    placed = (
        P(("row", "rep"), None),
        P(("row", "rep"), None, None, None),
        P(("row", "rep"), None),
        P(),
        P(),
        P(),
        P(),
        P(("row", "rep"), None),
    )
    return jax.shard_map(
        local,
        mesh=mesh,
        in_specs=placed,
        out_specs=(
            P(("row", "rep"), None),
            P(("row", "rep"), None),
            P("rep", None),
            P("rep", None),
            P("rep", None),
            P("rep", None),
        ),
        check_vma=False,
    )
```
